32 devices in a mesh: dp: 8 (over z, y), ep: 4 (over x, core).
Axes of the slice: x: 2, y: 2, z: 4, core: 2. Of those that a mesh axis runs over, the one named last changes fastest.
Arguments:
- grad: float32 [2, 1536, 3584], P(None, 'dp', 'ep'), may hold values from -40 to 40
- momentum: float32 [2, 1536, 3584], P(None, 'dp', 'ep'), may hold values from -6 to 6
- lengths: int32 [2, 8], replicated, may hold values from 1 to 192, 1024 in all within a row
Outputs:
- new_momentum: float32 [2, 1536, 3584], P(None, 'dp', 'ep')
- update: float32 [2, 1536, 3584], P(None, 'dp', 'ep')
The draws below stay inside these ranges and needn't reach their ends.
Inputs may be any that keep to these rules, and one draw needn't show every extreme that they name: lengths[j, d] counts the rows of matrix j held by dp index d, in order of d, in the first slots of its block of 192 slots; each row of lengths sums to 1024 and reaches 192.
All inputs are finite; a program needn't handle non-finite values.
Results may differ from the reference program's by a relative error of at most 0.009.
Values may be sent and summed in bfloat16 or wider, within the bound.
A program may use at most 64 MiB of HBM per device.

```python
import math
import jax
import jax.numpy as jnp
import numpy as np
from jax import lax

H = 1024
D = 3584
MATS = 2
RMAX = 192
SLOTS = 1536
N_DP = 8


def draw_grad(key, part):
    keys = jax.random.split(key, 3)
    shape = (MATS, SLOTS, D)
    row_scale = jnp.exp(jax.random.uniform(keys[1], (MATS, SLOTS, 1), jnp.float32) * math.log(10.0))
    col_scale = jnp.exp(jax.random.uniform(keys[2], (MATS, 1, D), jnp.float32) * math.log(10.0))
    base = jax.random.truncated_normal(keys[0], -4.0, 4.0, shape, jnp.float32)
    values = base * row_scale * col_scale / 10.0
    return values.astype(jnp.float32)


def levels(own_key, extent, pieces, low, top_value):
    def one(dim, shards_of):
        steps = jax.random.uniform(jax.random.fold_in(jax.random.fold_in(own_key, 6), dim), (shards_of,), jnp.float32, low / len(pieces), top_value / len(pieces))
        return jnp.repeat(jnp.exp(steps), extent[dim] // shards_of).reshape((-1,) + (1,) * (len(extent) - dim - 1))

    factor_of = one(*pieces[0])
    for cut in pieces[1:]:
        factor_of = factor_of * one(*cut)
    return factor_of


def length_profile(count, total, most, slope):
    weights = [(1 << 20) // math.isqrt(grade ** slope) + 1 for grade in range(2, count + 1)]
    rest, holding = total - most - (count - 1), [1] * (count - 1)
    while rest > 0:
        free = [i for i in range(count - 1) if holding[i] < most]
        whole, budget = sum([weights[i] for i in free]), rest
        for i in free:
            addition = min(most - holding[i], max(1, budget * weights[i] // whole), rest)
            holding[i] = holding[i] + addition
            rest = rest - addition
    return np.array([most] + holding)


def ragged_sizes(own_key, count, total, bound, slope):
    if count == 2:
        one = jax.random.randint(own_key, (), max(1, total - bound), min(bound, total - 1) + 1)
        return jnp.stack([one, total - one])
    tallies = jnp.asarray(length_profile(count, total, bound, slope), jnp.int32)
    couples = (count - 1) // 2
    source_of, sink = tallies[1:1 + 2 * couples:2], tallies[2:2 + 2 * couples:2]
    room = jnp.minimum(source_of - 1, bound - sink)
    moved = jax.random.randint(jax.random.fold_in(own_key, 1), (couples,), 0, 1 << 20) % (room + 1)
    tallies = tallies.at[1:1 + 2 * couples:2].set(source_of - moved).at[2:2 + 2 * couples:2].set(sink + moved)
    return tallies[jax.random.permutation(jax.random.fold_in(own_key, 2), count)]


def centred(own_key, dims, scale, most, cuts=(), held_as=jnp.bfloat16):
    values = jax.random.normal(own_key, dims, jnp.float32) * scale
    if len(cuts) > 0:
        values = levels(own_key, dims, cuts, -0.22, 0.18) * values
    return jnp.clip(values, min=-most, max=most).astype(held_as)


def setup_inputs(seed: int = 0) -> dict:
    arg_keys = jax.random.split(jax.random.key(seed), 4)
    return {
        "grad": draw_grad(jax.random.fold_in(arg_keys[3], 71), 0),
        "momentum": centred(arg_keys[1], (MATS, SLOTS, D), 1.0, 6.0, ((1, 8), (2, 4)), jnp.float32),
        "lengths": jax.vmap(lambda own: ragged_sizes(own, N_DP, H, RMAX, 2))(jax.random.split(arg_keys[2], MATS)).reshape((MATS, N_DP)).astype(jnp.int32),
    }


MOMENTUM_COEF = 0.95
EPSILON = 1e-06
FIRST_LIN = 3.0
FIRST_CUBE = -2.5
SECOND_LIN = 1.5
SECOND_CUBE = -0.5

def newton_polar(scaled_gram, factor, matrix):
    product = jnp.dot(scaled_gram, matrix, preferred_element_type=jnp.float32)
    first_iter = (factor * (FIRST_LIN * matrix.astype(jnp.float32) + FIRST_CUBE * product)).astype(jnp.bfloat16)
    product = jnp.dot(scaled_gram, first_iter, preferred_element_type=jnp.float32)
    applied = (FIRST_LIN * first_iter.astype(jnp.float32) + FIRST_CUBE * product).astype(jnp.bfloat16)
    second = jnp.dot(scaled_gram, applied, preferred_element_type=jnp.float32).astype(jnp.bfloat16)
    third = FIRST_LIN * second.astype(jnp.float32) + FIRST_CUBE * jnp.dot(scaled_gram, second, preferred_element_type=jnp.float32)
    return (SECOND_LIN * first_iter.astype(jnp.float32) + SECOND_CUBE * third).astype(jnp.bfloat16)

def reference(grad, momentum, lengths):
    new_momentum = MOMENTUM_COEF * momentum + grad
    rounded = (grad + MOMENTUM_COEF * new_momentum).astype(jnp.bfloat16)
    offsets = jnp.cumsum(lengths, axis=1) - lengths
    slot_ids = jnp.arange(SLOTS, dtype=jnp.int32)
    source = slot_ids // RMAX
    within = slot_ids % RMAX
    scale_out = math.sqrt(max(H, D))
    results = []
    for matrix_id in range(MATS):
        length_at = jnp.take(lengths[matrix_id], source)
        offset_at = jnp.take(offsets[matrix_id], source)
        is_valid = within < length_at
        target = jnp.where(is_valid, offset_at + within, H).astype(jnp.int32)
        matrix = jnp.zeros((H, D), jnp.bfloat16).at[target].set(rounded[matrix_id], mode='drop')
        gram = jnp.dot(matrix, matrix.T, preferred_element_type=jnp.float32)
        scale_sq = lax.rsqrt(jnp.sum(gram * gram) + EPSILON)
        scaled_gram = (scale_sq * gram).astype(jnp.bfloat16)
        ortho = newton_polar(scaled_gram, jnp.sqrt(scale_sq), matrix)
        picked = jnp.take(ortho, jnp.where(is_valid, target, 0).astype(jnp.int32), axis=0)
        results.append(jnp.where(is_valid[:, None], picked.astype(jnp.float32) * scale_out, jnp.float32(0.0)))
    return (new_momentum, jnp.stack(results))
```

```python
import functools
import math

import jax
import jax.numpy as jnp
from jax import lax
from jax.experimental import pallas as pl
from jax.experimental.pallas import tpu as pltpu
from jax.sharding import PartitionSpec as P

H = 1024
D = 3584


MOMENTUM_COEF = 0.95
EPSILON = 1e-06
FIRST_LIN = 3.0
FIRST_CUBE = -2.5
SECOND_LIN = 1.5
SECOND_CUBE = -0.5

LANES = 128
BLOCKS = 8
KEPT = BLOCKS // 2 + 1
MESH = pl.DeviceIdType.MESH
VMEM_LIMIT = 48 * 1024 * 1024


def from_root(block, axis, owner):
    block = jnp.where(lax.axis_index(axis) == owner, block, jnp.zeros_like(block))
    return lax.psum(block, axis)


def newton_polar(scaled_gram, factor, matrix):
    product = jnp.dot(scaled_gram, matrix, preferred_element_type=jnp.float32)
    first_iter = (factor * (FIRST_LIN * matrix.astype(jnp.float32) + FIRST_CUBE * product)).astype(
        jnp.bfloat16
    )
    product = jnp.dot(scaled_gram, first_iter, preferred_element_type=jnp.float32)
    applied = (FIRST_LIN * first_iter.astype(jnp.float32) + FIRST_CUBE * product).astype(
        jnp.bfloat16
    )
    second = jnp.dot(scaled_gram, applied, preferred_element_type=jnp.float32).astype(jnp.bfloat16)
    third = FIRST_LIN * second.astype(jnp.float32) + FIRST_CUBE * jnp.dot(
        scaled_gram, second, preferred_element_type=jnp.float32
    )
    return (SECOND_LIN * first_iter.astype(jnp.float32) + SECOND_CUBE * third).astype(jnp.bfloat16)


def gathered_body(grad, momentum, lengths):
    matrices = grad.shape[0]
    slot_rows = grad.shape[1]
    columns = grad.shape[2]
    new_momentum = MOMENTUM_COEF * momentum + grad
    rounded = (grad + MOMENTUM_COEF * new_momentum).astype(jnp.bfloat16)
    holders = lax.axis_size("dp")
    myself = lax.axis_index("dp")
    is_owner = myself < matrices
    chosen = jnp.minimum(myself, matrices - 1)
    offsets = jnp.cumsum(lengths, axis=1) - lengths
    chosen_len = lax.dynamic_index_in_dim(lengths, chosen, 0, keepdims=False)
    chosen_off = lax.dynamic_index_in_dim(offsets, chosen, 0, keepdims=False)
    device_ids = jnp.arange(holders, dtype=jnp.int32)
    portion = lax.all_gather(rounded, "dp", axis=1, tiled=True)
    piece_rows = portion.shape[1]
    incoming = lax.dynamic_index_in_dim(portion, chosen, 0, keepdims=False)
    slot_ids = jnp.arange(piece_rows, dtype=jnp.int32)
    source = slot_ids // slot_rows
    within = slot_ids % slot_rows
    matches = source[:, None] == device_ids[None, :]
    length_at = jnp.sum(jnp.where(matches, chosen_len[None, :], 0), axis=1)
    offset_at = jnp.sum(jnp.where(matches, chosen_off[None, :], 0), axis=1)
    keep = jnp.logical_and(within < length_at, is_owner)
    target = jnp.where(keep, offset_at + within, H)
    matrix = jnp.zeros((H, columns), jnp.bfloat16).at[target].set(incoming, mode="drop")
    portion = lax.all_gather(matrix, "ep", axis=1, tiled=True)
    gram_full = jnp.dot(portion, portion.T, preferred_element_type=jnp.float32)
    scale_sq = lax.rsqrt(jnp.sum(gram_full * gram_full) + EPSILON)
    scaled_gram = (scale_sq * gram_full).astype(jnp.bfloat16)
    ortho = newton_polar(scaled_gram, jnp.sqrt(scale_sq), matrix)
    scale_out = math.sqrt(max(H, D))
    positions = jnp.arange(slot_rows, dtype=jnp.int32)
    results = []
    for matrix_id in range(matrices):
        owned_ortho = from_root(ortho, "dp", matrix_id)
        own_length = lax.dynamic_index_in_dim(lengths[matrix_id], myself, 0, keepdims=False)
        own_offset = lax.dynamic_index_in_dim(offsets[matrix_id], myself, 0, keepdims=False)
        is_valid = positions < own_length
        picked = jnp.take(owned_ortho, jnp.where(is_valid, own_offset + positions, 0), axis=0)
        results.append(
            jnp.where(is_valid[:, None], picked.astype(jnp.float32) * scale_out, jnp.float32(0.0))
        )
    return (new_momentum, jnp.stack(results))


def far_first(count):
    return sorted(range(1, count), key=lambda r: abs(r - count // 2))


def meet(partners):
    barrier = pltpu.get_barrier_semaphore()
    for partner in partners:
        pl.semaphore_signal(barrier, inc=1, device_id=partner, device_id_type=MESH)
    pl.semaphore_wait(barrier, len(partners))


def other_core(ep):
    return ep + 1 - 2 * lax.rem(ep, 2)


def spread_kernel(holders, send_ref, held_ref, sent, landed, passed, got, local):
    me, ep = lax.axis_index("dp"), lax.axis_index("ep")
    sibling = (me, other_core(ep))
    meet([(lax.rem(me + r, holders), ep) for r in range(1, holders)] + [sibling])

    copies = {}
    for r in far_first(holders):
        to = lax.rem(me + r, holders)
        copies[r] = pltpu.make_async_remote_copy(
            src_ref=send_ref.at[to],
            dst_ref=held_ref.at[0, me],
            send_sem=sent.at[r],
            recv_sem=landed.at[r],
            device_id=(to, ep),
            device_id_type=MESH,
        )
        copies[r].start()
    own = pltpu.make_async_copy(send_ref.at[me], held_ref.at[0, me], local)
    own.start()
    forwards = [
        pltpu.make_async_remote_copy(
            src_ref=send_ref.at[me],
            dst_ref=held_ref.at[1, me],
            send_sem=passed.at[0],
            recv_sem=got.at[0],
            device_id=sibling,
            device_id_type=MESH,
        )
    ]
    forwards[0].start()
    for r in reversed(far_first(holders)):
        source = lax.rem(me + holders - r, holders)
        copies[r].wait_recv()
        forward = pltpu.make_async_remote_copy(
            src_ref=held_ref.at[0, source],
            dst_ref=held_ref.at[1, source],
            send_sem=passed.at[r],
            recv_sem=got.at[r],
            device_id=sibling,
            device_id_type=MESH,
        )
        forward.start()
        forwards.append(forward)
    own.wait()
    for r in far_first(holders):
        copies[r].wait_send()
    for forward in forwards:
        forward.wait()


def spread(chunks):
    holders = chunks.shape[0]
    dma = pltpu.SemaphoreType.DMA
    return pl.pallas_call(
        functools.partial(spread_kernel, holders),
        out_shape=jax.ShapeDtypeStruct((2,) + chunks.shape, chunks.dtype),
        in_specs=[pl.BlockSpec(memory_space=pl.ANY)],
        out_specs=pl.BlockSpec(memory_space=pl.ANY),
        scratch_shapes=[dma((holders,)), dma((holders,)), dma((holders,)), dma((holders,)), dma],
        compiler_params=pltpu.CompilerParams(collective_id=0, has_side_effects=True),
        name="spread",
    )(chunks)


def collect_kernel(holders, send_ref, held_ref, sent, landed, local):
    me, ep = lax.axis_index("dp"), lax.axis_index("ep")
    meet([(lax.rem(me + r, holders), ep) for r in range(1, holders)])
    copies = []
    for r in far_first(holders):
        to = lax.rem(me + r, holders)
        copy = pltpu.make_async_remote_copy(
            src_ref=send_ref.at[to],
            dst_ref=held_ref.at[me],
            send_sem=sent.at[r],
            recv_sem=landed.at[r],
            device_id=(to, ep),
            device_id_type=MESH,
        )
        copy.start()
        copies.append(copy)
    own = pltpu.make_async_copy(send_ref.at[me], held_ref.at[me], local)
    own.start()
    own.wait()
    for copy in copies:
        copy.wait()


def collect(chunks):
    holders = chunks.shape[0]
    dma = pltpu.SemaphoreType.DMA
    return pl.pallas_call(
        functools.partial(collect_kernel, holders),
        out_shape=jax.ShapeDtypeStruct(chunks.shape, chunks.dtype),
        in_specs=[pl.BlockSpec(memory_space=pl.ANY)],
        out_specs=pl.BlockSpec(memory_space=pl.ANY),
        scratch_shapes=[dma((holders,)), dma((holders,)), dma],
        compiler_params=pltpu.CompilerParams(collective_id=1, has_side_effects=True),
        name="collect",
    )(chunks)


def reduce_kernel(
    group, peers, parts_ref, whole_ref, terms, reduced, sent, landed, out, into, passed, got, local
):
    dp, ep = lax.axis_index("dp"), lax.axis_index("ep")
    chips = peers // group
    base, core = dp - lax.rem(dp, group), lax.rem(ep, 2)
    me = lax.rem(dp, group) * chips + ep // 2
    sibling = (dp, other_core(ep))

    def device(index):
        return (base + index // chips, lax.rem(index, chips) * 2 + core)

    meet([device(lax.rem(me + r, peers)) for r in range(1, peers)] + [sibling])

    copies = []
    for r in range(1, peers):
        to = lax.rem(me + r, peers)
        copy = pltpu.make_async_remote_copy(
            src_ref=parts_ref.at[to],
            dst_ref=terms.at[r],
            send_sem=sent.at[r],
            recv_sem=landed.at[r],
            device_id=device(to),
            device_id_type=MESH,
        )
        copy.start()
        copies.append(copy)
    total = parts_ref[me].astype(jnp.float32)
    for r in range(1, peers):
        copies[r - 1].wait_recv()
        total = total + terms[r].astype(jnp.float32)
    reduced[...] = total.astype(reduced.dtype)

    spreads = []
    for r in range(1, peers):
        copy = pltpu.make_async_remote_copy(
            src_ref=reduced,
            dst_ref=whole_ref.at[0, me],
            send_sem=out.at[r],
            recv_sem=into.at[r],
            device_id=device(lax.rem(me + r, peers)),
            device_id_type=MESH,
        )
        copy.start()
        spreads.append(copy)
    own = pltpu.make_async_copy(reduced, whole_ref.at[0, me], local)
    own.start()
    forwards = [
        pltpu.make_async_remote_copy(
            src_ref=reduced,
            dst_ref=whole_ref.at[1, me],
            send_sem=passed.at[0],
            recv_sem=got.at[0],
            device_id=sibling,
            device_id_type=MESH,
        )
    ]
    forwards[0].start()
    for r in range(1, peers):
        source = lax.rem(me + peers - r, peers)
        spreads[r - 1].wait_recv()
        forward = pltpu.make_async_remote_copy(
            src_ref=whole_ref.at[0, source],
            dst_ref=whole_ref.at[1, source],
            send_sem=passed.at[r],
            recv_sem=got.at[r],
            device_id=sibling,
            device_id_type=MESH,
        )
        forward.start()
        forwards.append(forward)
    own.wait()
    for copy in copies:
        copy.wait_send()
    for copy in spreads:
        copy.wait_send()
    for forward in forwards:
        forward.wait()


def reduce_parts(parts, group):
    peers = parts.shape[0]
    dma = pltpu.SemaphoreType.DMA
    return pl.pallas_call(
        functools.partial(reduce_kernel, group, peers),
        out_shape=jax.ShapeDtypeStruct((2,) + parts.shape, parts.dtype),
        in_specs=[pl.BlockSpec(memory_space=pltpu.VMEM)],
        out_specs=pl.BlockSpec(memory_space=pl.ANY),
        scratch_shapes=[
            pltpu.VMEM(parts.shape, parts.dtype),
            pltpu.VMEM(parts.shape[1:], parts.dtype),
        ]
        + [dma((peers,))] * 6
        + [dma],
        compiler_params=pltpu.CompilerParams(
            collective_id=2, has_side_effects=True, vmem_limit_bytes=VMEM_LIMIT
        ),
        name="reduce_parts",
    )(parts)


def gram_kernel(target_ref, held_ref, matrix_ref, parts_ref, both):
    height, width = matrix_ref.shape
    slots = held_ref.shape[1]
    tile = 256
    target = target_ref[...]

    def pack(step, carry):
        start = pl.multiple_of(step * tile, tile)
        rows = lax.broadcasted_iota(jnp.int32, (tile, slots), 0) + start
        chosen = jnp.where(rows == target, 1.0, 0.0).astype(jnp.bfloat16)
        mine = jnp.dot(chosen, held_ref[0], preferred_element_type=jnp.float32)
        mine = mine.astype(jnp.bfloat16)
        matrix_ref[pl.ds(start, tile), :] = mine
        both[pl.ds(start, tile), :width] = mine
        theirs = jnp.dot(chosen, held_ref[1], preferred_element_type=jnp.float32)
        both[pl.ds(start, tile), width:] = theirs.astype(jnp.bfloat16)
        return carry

    lax.fori_loop(0, height // tile, pack, 0)
    block = height // BLOCKS

    def multiply(step, carry):
        start = pl.multiple_of(step * block, block)
        part = lax.dot_general(
            both[pl.ds(start, block), :],
            both[pl.ds(start, KEPT * block), :],
            (((1,), (1,)), ((), ())),
            preferred_element_type=jnp.float32,
        )
        parts_ref[pl.ds(start, block), :] = part.astype(jnp.bfloat16)
        return carry

    lax.fori_loop(0, BLOCKS // 2, multiply, 0)


def local_gram(target, held):
    width = held.shape[2]
    return pl.pallas_call(
        gram_kernel,
        out_shape=(
            jax.ShapeDtypeStruct((H, width), jnp.bfloat16),
            jax.ShapeDtypeStruct((H // 2, KEPT * (H // BLOCKS)), jnp.bfloat16),
        ),
        scratch_shapes=[pltpu.VMEM((H, 2 * width), jnp.bfloat16)],
        compiler_params=pltpu.CompilerParams(vmem_limit_bytes=VMEM_LIMIT),
        name="local_gram",
    )(target, held)


def chain_kernel(slot_rows, target_ref, blocks_ref, matrix_ref, slots_ref, gram, first, applied):
    height, width = matrix_ref.shape
    block = height // BLOCKS
    squares = jnp.zeros((8, LANES), jnp.float32)
    for i in range(BLOCKS):
        for k in range(KEPT):
            piece = blocks_ref[pl.ds(i * block, block), pl.ds(k * block, block)]
            j = (i + k) % BLOCKS
            gram[pl.ds(i * block, block), pl.ds(j * block, block)] = piece
            wide = piece.astype(jnp.float32)
            if 0 < k < BLOCKS - KEPT + 1:
                gram[pl.ds(j * block, block), pl.ds(i * block, block)] = wide.T.astype(jnp.bfloat16)
            weight = 2.0 if 0 < k < BLOCKS - KEPT + 1 else 1.0
            square = (wide * wide).reshape(-1, 8, block).sum(axis=0)
            for lane in range(block // LANES):
                squares = squares + weight * square[:, lane * LANES : (lane + 1) * LANES]
    scale_sq = lax.rsqrt(jnp.sum(squares, keepdims=True) + EPSILON)
    factor = jnp.sqrt(scale_sq)
    tile = 256
    steps = height // tile

    def product(start, right):
        return scale_sq * jnp.dot(
            gram[pl.ds(start, tile), :], right[...], preferred_element_type=jnp.float32
        )

    def each(step):
        def run(index, carry):
            step(pl.multiple_of(index * tile, tile))
            return carry

        lax.fori_loop(0, steps, run, 0)

    def one(start):
        rows = matrix_ref[pl.ds(start, tile), :].astype(jnp.float32)
        value = factor * (FIRST_LIN * rows + FIRST_CUBE * product(start, matrix_ref))
        first[pl.ds(start, tile), :] = value.astype(jnp.bfloat16)

    def two(start):
        rows = first[pl.ds(start, tile), :].astype(jnp.float32)
        value = FIRST_LIN * rows + FIRST_CUBE * product(start, first)
        applied[0, pl.ds(start, tile), :] = value.astype(jnp.bfloat16)

    def three(start):
        value = product(start, applied.at[0])
        applied[1, pl.ds(start, tile), :] = value.astype(jnp.bfloat16)

    def four(start):
        rows = applied[1, pl.ds(start, tile), :].astype(jnp.float32)
        third = FIRST_LIN * rows + FIRST_CUBE * product(start, applied.at[1])
        rows = first[pl.ds(start, tile), :].astype(jnp.float32)
        value = SECOND_LIN * rows + SECOND_CUBE * third
        applied[0, pl.ds(start, tile), :] = value.astype(jnp.bfloat16)

    for step in (one, two, three, four):
        each(step)

    def lay_out(index, carry):
        start = pl.multiple_of(index * slot_rows, slot_rows)
        wanted = lax.broadcasted_iota(jnp.int32, (slot_rows, height), 1)
        chosen = jnp.where(wanted == target_ref[pl.ds(start, slot_rows), :], 1.0, 0.0)
        rows = jnp.dot(
            chosen.astype(jnp.bfloat16), applied[0], preferred_element_type=jnp.float32
        )
        slots_ref[pl.ds(start, slot_rows), :] = rows.astype(jnp.bfloat16)
        return carry

    lax.fori_loop(0, slots_ref.shape[0] // slot_rows, lay_out, 0)


def apply_chain(target, blocks, matrix, slot_rows):
    width = matrix.shape[1]
    return pl.pallas_call(
        functools.partial(chain_kernel, slot_rows),
        out_shape=jax.ShapeDtypeStruct((target.shape[0], width), jnp.bfloat16),
        scratch_shapes=[
            pltpu.VMEM((H, H), jnp.bfloat16),
            pltpu.VMEM((H, width), jnp.bfloat16),
            pltpu.VMEM((2, H, width), jnp.bfloat16),
        ],
        compiler_params=pltpu.CompilerParams(vmem_limit_bytes=VMEM_LIMIT),
        name="apply_chain",
    )(target, blocks, matrix)


def chunk_width(columns, group):
    return -(-columns // (group * LANES)) * LANES


def split_body(grad, momentum, lengths):
    matrices, slot_rows, columns = grad.shape
    holders = lax.axis_size("dp")
    group = holders // matrices
    width = chunk_width(columns, group)
    peers = group * (lax.axis_size("ep") // 2)
    new_momentum = MOMENTUM_COEF * momentum + grad
    rounded = (grad + MOMENTUM_COEF * new_momentum).astype(jnp.bfloat16)
    chunks = jnp.pad(rounded, ((0, 0), (0, 0), (0, group * width - columns)))
    chunks = chunks.reshape(matrices, slot_rows, group, width).transpose(0, 2, 1, 3)
    chunks = chunks.reshape(holders, slot_rows, width)

    chosen = lax.axis_index("dp") // group
    own_lengths = lax.dynamic_index_in_dim(lengths, chosen, 0, keepdims=False)
    own_offsets = jnp.cumsum(own_lengths) - own_lengths
    within = jnp.arange(slot_rows, dtype=jnp.int32)[None, :]
    row = own_offsets[:, None] + within
    row = (row + lax.rem(lax.axis_index("ep"), 2) * (H // 2)) % H
    target = jnp.where(within < own_lengths[:, None], row, -1).reshape(-1)

    held = spread(chunks).reshape(2, holders * slot_rows, width)
    matrix, parts = local_gram(target[None, :], held)
    blocks = reduce_parts(parts.reshape(peers, -1, parts.shape[1]), group)
    ortho = apply_chain(target[:, None], blocks.reshape(H, -1), matrix, slot_rows)
    back = collect(ortho.reshape(holders, slot_rows, width))
    back = back.reshape(matrices, group, slot_rows, width).transpose(0, 2, 1, 3)
    back = back.reshape(matrices, slot_rows, group * width)[:, :, :columns]
    return (new_momentum, back.astype(jnp.float32) * math.sqrt(max(H, D)))


def can_split(holders, shards, matrices, slot_rows, columns):
    if holders % matrices or shards % 2 or slot_rows % 16:
        return False
    group = holders // matrices
    if group * chunk_width(columns, group) * 3 > columns * 4:
        return False
    return H % (BLOCKS * LANES) == 0 and H // 2 % (group * (shards // 2) * 16) == 0


def solution(mesh):
    def run(grad, momentum, lengths):
        matrices, slots, columns = grad.shape
        holders, shards = mesh.shape["dp"], mesh.shape["ep"]
        fits = can_split(holders, shards, matrices, slots // holders, columns // shards)
        return jax.shard_map(
            split_body if fits else gathered_body,
            mesh=mesh,
            in_specs=(P(None, "dp", "ep"), P(None, "dp", "ep"), P()),
            out_specs=(P(None, "dp", "ep"), P(None, "dp", "ep")),
            check_vma=False,
        )(grad, momentum, lengths)

    return run
```

```python
import functools
import math

import jax
import jax.numpy as jnp
from jax import lax
from jax.experimental import pallas as pl
from jax.experimental.pallas import tpu as pltpu
from jax.sharding import PartitionSpec as P

H = 1024
D = 3584


MOMENTUM_COEF = 0.95
EPSILON = 1e-06
FIRST_LIN = 3.0
FIRST_CUBE = -2.5
SECOND_LIN = 1.5
SECOND_CUBE = -0.5

LANES = 128
BLOCKS = 8
KEPT = BLOCKS // 2 + 1
MESH = pl.DeviceIdType.MESH
VMEM_LIMIT = 48 * 1024 * 1024


def from_root(block, axis, owner):
    block = jnp.where(lax.axis_index(axis) == owner, block, jnp.zeros_like(block))
    return lax.psum(block, axis)


def newton_polar(scaled_gram, factor, matrix):
    product = jnp.dot(scaled_gram, matrix, preferred_element_type=jnp.float32)
    first_iter = (factor * (FIRST_LIN * matrix.astype(jnp.float32) + FIRST_CUBE * product)).astype(
        jnp.bfloat16
    )
    product = jnp.dot(scaled_gram, first_iter, preferred_element_type=jnp.float32)
    applied = (FIRST_LIN * first_iter.astype(jnp.float32) + FIRST_CUBE * product).astype(
        jnp.bfloat16
    )
    second = jnp.dot(scaled_gram, applied, preferred_element_type=jnp.float32).astype(jnp.bfloat16)
    third = FIRST_LIN * second.astype(jnp.float32) + FIRST_CUBE * jnp.dot(
        scaled_gram, second, preferred_element_type=jnp.float32
    )
    return (SECOND_LIN * first_iter.astype(jnp.float32) + SECOND_CUBE * third).astype(jnp.bfloat16)


def gathered_body(grad, momentum, lengths):
    matrices = grad.shape[0]
    slot_rows = grad.shape[1]
    columns = grad.shape[2]
    new_momentum = MOMENTUM_COEF * momentum + grad
    rounded = (grad + MOMENTUM_COEF * new_momentum).astype(jnp.bfloat16)
    holders = lax.axis_size("dp")
    myself = lax.axis_index("dp")
    is_owner = myself < matrices
    chosen = jnp.minimum(myself, matrices - 1)
    offsets = jnp.cumsum(lengths, axis=1) - lengths
    chosen_len = lax.dynamic_index_in_dim(lengths, chosen, 0, keepdims=False)
    chosen_off = lax.dynamic_index_in_dim(offsets, chosen, 0, keepdims=False)
    device_ids = jnp.arange(holders, dtype=jnp.int32)
    portion = lax.all_gather(rounded, "dp", axis=1, tiled=True)
    piece_rows = portion.shape[1]
    incoming = lax.dynamic_index_in_dim(portion, chosen, 0, keepdims=False)
    slot_ids = jnp.arange(piece_rows, dtype=jnp.int32)
    source = slot_ids // slot_rows
    within = slot_ids % slot_rows
    matches = source[:, None] == device_ids[None, :]
    length_at = jnp.sum(jnp.where(matches, chosen_len[None, :], 0), axis=1)
    offset_at = jnp.sum(jnp.where(matches, chosen_off[None, :], 0), axis=1)
    keep = jnp.logical_and(within < length_at, is_owner)
    target = jnp.where(keep, offset_at + within, H)
    matrix = jnp.zeros((H, columns), jnp.bfloat16).at[target].set(incoming, mode="drop")
    portion = lax.all_gather(matrix, "ep", axis=1, tiled=True)
    gram_full = jnp.dot(portion, portion.T, preferred_element_type=jnp.float32)
    scale_sq = lax.rsqrt(jnp.sum(gram_full * gram_full) + EPSILON)
    scaled_gram = (scale_sq * gram_full).astype(jnp.bfloat16)
    ortho = newton_polar(scaled_gram, jnp.sqrt(scale_sq), matrix)
    scale_out = math.sqrt(max(H, D))
    positions = jnp.arange(slot_rows, dtype=jnp.int32)
    results = []
    for matrix_id in range(matrices):
        owned_ortho = from_root(ortho, "dp", matrix_id)
        own_length = lax.dynamic_index_in_dim(lengths[matrix_id], myself, 0, keepdims=False)
        own_offset = lax.dynamic_index_in_dim(offsets[matrix_id], myself, 0, keepdims=False)
        is_valid = positions < own_length
        picked = jnp.take(owned_ortho, jnp.where(is_valid, own_offset + positions, 0), axis=0)
        results.append(
            jnp.where(is_valid[:, None], picked.astype(jnp.float32) * scale_out, jnp.float32(0.0))
        )
    return (new_momentum, jnp.stack(results))


def other_core(ep):
    return ep + 1 - 2 * lax.rem(ep, 2)


def rows_at(index, count):
    return pl.ds(pl.multiple_of(index * count, count), count)


def step_kernel(
    holders,
    shards,
    lengths_ref,
    grad_ref,
    momentum_ref,
    back_ref,
    rounded,
    held,
    both,
    parts,
    terms,
    reduced,
    gram,
    first,
    applied,
    slots,
    chunk_sems,
    core_sems,
    term_sems,
    block_sems,
    half_sems,
    slot_sems,
    local,
):
    matrices, slot_rows, columns = grad_ref.shape
    group = holders // matrices
    chips = shards // 2
    peers = group * chips
    width = held.shape[2]
    narrow = columns - (group - 1) * width
    height = both.shape[0]
    block = height // BLOCKS
    part_rows = height // 2 // peers
    span = KEPT * block

    dp, ep = lax.axis_index("dp"), lax.axis_index("ep")
    core = lax.rem(ep, 2)
    mine = dp // group
    place = lax.rem(dp, group)
    base = dp - place
    sibling = (dp, other_core(ep))

    def chunk_of(index, core):
        return lax.rem(index + core, group)

    def with_width(chunk, use):
        @pl.when(chunk < group - 1)
        def _():
            use(width)

        @pl.when(chunk == group - 1)
        def _():
            use(narrow)

    own_chunk = chunk_of(place, core)
    sibling_chunk = chunk_of(place, 1 - core)

    partners = [(lax.rem(dp + r, holders), ep) for r in range(1, holders)] + [sibling]
    for chip in range(1, chips):
        other = lax.rem(ep // 2 + chip, chips) * 2 + core
        partners += [(base + k, other) for k in range(group)]

    if narrow < width:
        held[:, :, narrow:] = jnp.zeros((2, held.shape[1], width - narrow), held.dtype)
    barrier = pltpu.get_barrier_semaphore()
    for partner in partners:
        pl.semaphore_signal(barrier, inc=1, device_id=partner, device_id_type=MESH)

    def round_rows(j):
        momentum = MOMENTUM_COEF * momentum_ref[j] + grad_ref[j]
        rounded[j] = (grad_ref[j] + MOMENTUM_COEF * momentum).astype(rounded.dtype)

    def chunk_copy(to, r, w):
        start = pl.multiple_of(chunk_of(lax.rem(to, group), core) * width, LANES)
        return pltpu.make_async_remote_copy(
            src_ref=rounded.at[to // group, :, pl.ds(start, w)],
            dst_ref=held.at[0, rows_at(dp, slot_rows), pl.ds(0, w)],
            send_sem=chunk_sems.at[0, r],
            recv_sem=chunk_sems.at[1, r],
            device_id=(to, ep),
            device_id_type=MESH,
        )

    def core_copy(source, r, w):
        return pltpu.make_async_remote_copy(
            src_ref=held.at[0, rows_at(source, slot_rows), pl.ds(0, w)],
            dst_ref=held.at[1, rows_at(source, slot_rows), pl.ds(0, w)],
            send_sem=core_sems.at[0, r],
            recv_sem=core_sems.at[1, r],
            device_id=sibling,
            device_id_type=MESH,
        )

    round_rows(lax.rem(mine + 1, matrices))
    pl.semaphore_wait(barrier, len(partners))
    order = []
    for t in range(1, matrices + 1):
        if t > 1:
            round_rows(lax.rem(mine + t, matrices))
        for k in range(group):
            if t == matrices and k == 0:
                continue
            order.append((t % matrices) * group + k)
            to = lax.rem(mine + t, matrices) * group + lax.rem(place + k, group)
            r = order[-1]
            chunk = chunk_of(lax.rem(to, group), core)
            with_width(chunk, lambda w, to=to, r=r: chunk_copy(to, r, w).start())

    def own_move(w):
        start = pl.multiple_of(own_chunk * width, LANES)
        move = pltpu.make_async_copy(
            rounded.at[mine, :, pl.ds(start, w)],
            held.at[0, rows_at(dp, slot_rows), pl.ds(0, w)],
            local,
        )
        move.start()
        move.wait()

    with_width(own_chunk, own_move)
    with_width(own_chunk, lambda w: core_copy(dp, 0, w).start())

    def source_of(r):
        t, k = r // group, r % group
        half = lax.rem(mine + matrices - t, matrices)
        return half * group + lax.rem(place + group - k, group)

    arrivals = [r for r in order if r < group] + [r for r in order if r >= group]
    for r in arrivals:

        def pass_on(w, r=r):
            chunk_copy(dp, r, w).wait_recv()
            core_copy(source_of(r), r, w).start()

        with_width(own_chunk, pass_on)
    for r in [0] + arrivals:
        with_width(sibling_chunk, lambda w, r=r: core_copy(dp, r, w).wait_recv())

    total_slots = holders * slot_rows
    slot = lax.broadcasted_iota(jnp.int32, (1, total_slots), 1)
    target = jnp.full((1, total_slots), -1, jnp.int32)
    offset = core * (height // 2)
    for d in range(holders):
        live = lengths_ref[mine, d]
        inside = jnp.logical_and(slot >= d * slot_rows, slot < d * slot_rows + live)
        row = slot - d * slot_rows + offset
        target = jnp.where(inside, jnp.where(row >= height, row - height, row), target)
        offset = offset + live

    tile = 256

    def pack(step, carry):
        start = pl.multiple_of(step * tile, tile)
        rows = lax.broadcasted_iota(jnp.int32, (tile, total_slots), 0) + start
        chosen = jnp.where(rows == target, 1.0, 0.0).astype(jnp.bfloat16)
        for which in range(2):
            packed = jnp.dot(chosen, held[which], preferred_element_type=jnp.float32)
            both[pl.ds(start, tile), which * width : (which + 1) * width] = packed.astype(
                jnp.bfloat16
            )
        return carry

    lax.fori_loop(0, height // tile, pack, 0)

    me = place * chips + ep // 2

    def device(index):
        return (base + index // chips, lax.rem(index, chips) * 2 + core)

    def term_copy(to, r):
        return pltpu.make_async_remote_copy(
            src_ref=parts.at[rows_at(to, part_rows)],
            dst_ref=terms.at[r],
            send_sem=term_sems.at[0, r],
            recv_sem=term_sems.at[1, r],
            device_id=device(to),
            device_id_type=MESH,
        )

    def multiply(step, carry):
        start = pl.multiple_of(step * block, block)
        part = lax.dot_general(
            both[pl.ds(start, block), :],
            both[pl.ds(start, span), :],
            (((1,), (1,)), ((), ())),
            preferred_element_type=jnp.float32,
        )
        parts[pl.ds(start, block), :] = part.astype(jnp.bfloat16)
        return carry

    lax.fori_loop(0, BLOCKS // 2, multiply, 0)
    for r in range(1, peers):
        term_copy(lax.rem(me + r, peers), r).start()
    total = parts[rows_at(me, part_rows), :].astype(jnp.float32)
    for r in range(1, peers):
        term_copy(me, r).wait_recv()
        total = total + terms[r].astype(jnp.float32)
    reduced[...] = total.astype(reduced.dtype)

    def blocks_at(index, half):
        row = half * (height // 2) + index * part_rows
        column = pl.multiple_of(row // block * block, block)
        return gram.at[pl.ds(pl.multiple_of(row, part_rows), part_rows), pl.ds(column, span)]

    def block_copy(to, r):
        return pltpu.make_async_remote_copy(
            src_ref=reduced,
            dst_ref=blocks_at(me, 0),
            send_sem=block_sems.at[0, r],
            recv_sem=block_sems.at[1, r],
            device_id=device(to),
            device_id_type=MESH,
        )

    def half_copy(source, r):
        return pltpu.make_async_remote_copy(
            src_ref=reduced if r == 0 else blocks_at(source, 0),
            dst_ref=blocks_at(source, 1),
            send_sem=half_sems.at[0, r],
            recv_sem=half_sems.at[1, r],
            device_id=sibling,
            device_id_type=MESH,
        )

    for r in range(1, peers):
        block_copy(lax.rem(me + r, peers), r).start()
    half_copy(me, 0).start()
    own = pltpu.make_async_copy(reduced, blocks_at(me, 0), local)
    own.start()
    for r in range(1, peers):
        block_copy(me, r).wait_recv()
        half_copy(lax.rem(me + peers - r, peers), r).start()
    own.wait()

    squares = jnp.zeros((8, LANES), jnp.float32)
    for i in range(BLOCKS):
        if i == BLOCKS // 2:
            for r in range(peers):
                half_copy(me, r).wait_recv()
        for k in range(KEPT):
            j = (i + k) % BLOCKS
            piece = gram[pl.ds(i * block, block), pl.ds((i + k) * block, block)]
            if i + k >= BLOCKS:
                gram[pl.ds(i * block, block), pl.ds(j * block, block)] = piece
            wide = piece.astype(jnp.float32)
            twice = 0 < k < BLOCKS - KEPT + 1
            if twice:
                gram[pl.ds(j * block, block), pl.ds(i * block, block)] = wide.T.astype(jnp.bfloat16)
            square = (wide * wide).reshape(-1, 8, block).sum(axis=0)
            for lane in range(block // LANES):
                squares = squares + (2.0 if twice else 1.0) * square[
                    :, lane * LANES : (lane + 1) * LANES
                ]
    scale_sq = lax.rsqrt(jnp.sum(squares, keepdims=True) + EPSILON)
    factor = jnp.sqrt(scale_sq)

    def product(start, right):
        return scale_sq * jnp.dot(
            gram[pl.ds(start, tile), :height], right, preferred_element_type=jnp.float32
        )

    def each(step):
        def run(index, carry):
            step(pl.multiple_of(index * tile, tile))
            return carry

        lax.fori_loop(0, height // tile, run, 0)

    def one(start):
        rows = both[pl.ds(start, tile), :width].astype(jnp.float32)
        value = factor * (FIRST_LIN * rows + FIRST_CUBE * product(start, both[:, :width]))
        first[pl.ds(start, tile), :] = value.astype(jnp.bfloat16)

    def two(start):
        rows = first[pl.ds(start, tile), :].astype(jnp.float32)
        value = FIRST_LIN * rows + FIRST_CUBE * product(start, first[...])
        applied[0, pl.ds(start, tile), :] = value.astype(jnp.bfloat16)

    def three(start):
        value = product(start, applied[0])
        applied[1, pl.ds(start, tile), :] = value.astype(jnp.bfloat16)

    def four(start):
        rows = applied[1, pl.ds(start, tile), :].astype(jnp.float32)
        third = FIRST_LIN * rows + FIRST_CUBE * product(start, applied[1])
        rows = first[pl.ds(start, tile), :].astype(jnp.float32)
        value = SECOND_LIN * rows + SECOND_CUBE * third
        applied[0, pl.ds(start, tile), :] = value.astype(jnp.bfloat16)

    for step in (one, two, three, four):
        each(step)

    def slot_copy(to, r, w):
        start = pl.multiple_of(own_chunk * width, LANES)
        return pltpu.make_async_remote_copy(
            src_ref=slots.at[rows_at(to, slot_rows), pl.ds(0, w)],
            dst_ref=back_ref.at[mine, :, pl.ds(start, w)],
            send_sem=slot_sems.at[0, r],
            recv_sem=slot_sems.at[1, r],
            device_id=(to, ep),
            device_id_type=MESH,
        )

    def incoming(r, w):
        source = source_of(r)
        start = pl.multiple_of(chunk_of(lax.rem(source, group), core) * width, LANES)
        return pltpu.make_async_remote_copy(
            src_ref=slots.at[rows_at(source, slot_rows), pl.ds(0, w)],
            dst_ref=back_ref.at[source // group, :, pl.ds(start, w)],
            send_sem=slot_sems.at[0, r],
            recv_sem=slot_sems.at[1, r],
            device_id=(source, ep),
            device_id_type=MESH,
        )

    def lay_out(to):
        start = core * (height // 2)
        live = lengths_ref[mine, to]
        for d in range(holders):
            start = start + jnp.where(d < to, lengths_ref[mine, d], 0)
        slot = lax.broadcasted_iota(jnp.int32, (slot_rows, height), 0)
        column = lax.broadcasted_iota(jnp.int32, (slot_rows, height), 1)
        row = slot + start
        row = jnp.where(row >= height, row - height, row)
        row = jnp.where(row >= height, row - height, row)
        chosen = jnp.where(jnp.logical_and(row == column, slot < live), 1.0, 0.0)
        rows = jnp.dot(
            chosen.astype(jnp.bfloat16), applied[0], preferred_element_type=jnp.float32
        )
        slots[rows_at(to, slot_rows), :] = rows.astype(jnp.bfloat16)

    def target_of(r):
        t, k = r // group, r % group
        return lax.rem(mine + t, matrices) * group + lax.rem(place + k, group)

    for r in order:
        to = target_of(r)
        lay_out(to)
        with_width(own_chunk, lambda w, to=to, r=r: slot_copy(to, r, w).start())
    lay_out(dp)

    def keep(w):
        start = pl.multiple_of(own_chunk * width, LANES)
        move = pltpu.make_async_copy(
            slots.at[rows_at(dp, slot_rows), pl.ds(0, w)],
            back_ref.at[mine, :, pl.ds(start, w)],
            local,
        )
        move.start()
        move.wait()

    with_width(own_chunk, keep)

    for r in order:
        to = target_of(r)
        chunk = chunk_of(lax.rem(to, group), core)
        with_width(chunk, lambda w, to=to, r=r: chunk_copy(to, r, w).wait_send())
    for r in [0] + order:
        with_width(own_chunk, lambda w, r=r: core_copy(dp, r, w).wait_send())
    for r in range(1, peers):
        term_copy(me, r).wait_send()
        block_copy(me, r).wait_send()
    for r in range(peers):
        half_copy(me, r).wait_send()
    for r in order:
        with_width(own_chunk, lambda w, r=r: slot_copy(dp, r, w).wait_send())
        chunk = chunk_of(lax.rem(source_of(r), group), core)
        with_width(chunk, lambda w, r=r: incoming(r, w).wait_recv())


def orthogonalize(grad, momentum, lengths):
    matrices, slot_rows, columns = grad.shape
    holders, shards = lax.axis_size("dp"), lax.axis_size("ep")
    group = holders // matrices
    peers = group * (shards // 2)
    width = chunk_width(columns, group)
    block = H // BLOCKS
    part = (H // 2 // peers, KEPT * block)
    held = (2, holders * slot_rows, width)
    dma = pltpu.SemaphoreType.DMA
    vmem = pl.BlockSpec(memory_space=pltpu.VMEM)

    def buffer(*shape):
        return pltpu.VMEM(shape, jnp.bfloat16)

    return pl.pallas_call(
        functools.partial(step_kernel, holders, shards),
        out_shape=jax.ShapeDtypeStruct(grad.shape, jnp.bfloat16),
        in_specs=[pl.BlockSpec(memory_space=pltpu.SMEM), vmem, vmem],
        out_specs=pl.BlockSpec(memory_space=pl.ANY),
        scratch_shapes=[
            buffer(*grad.shape),
            buffer(*held),
            buffer(H, 2 * width),
            buffer(H // 2, KEPT * block),
            buffer(peers, *part),
            buffer(*part),
            buffer(H, H + (KEPT - 1) * block),
            buffer(H, width),
            buffer(2, H, width),
            buffer(holders * slot_rows, width),
            dma((2, holders)),
            dma((2, holders)),
            dma((2, peers)),
            dma((2, peers)),
            dma((2, peers)),
            dma((2, holders)),
            dma,
        ],
        compiler_params=pltpu.CompilerParams(
            collective_id=0, has_side_effects=True, vmem_limit_bytes=VMEM_LIMIT
        ),
        name="orthogonalize",
    )(lengths, grad, momentum)


def chunk_width(columns, group):
    return -(-columns // (group * LANES)) * LANES


def split_body(grad, momentum, lengths):
    new_momentum = MOMENTUM_COEF * momentum + grad
    back = orthogonalize(grad, momentum, lengths)
    return (new_momentum, back.astype(jnp.float32) * math.sqrt(max(H, D)))


def can_split(holders, shards, matrices, slot_rows, columns):
    if holders % matrices or shards % 2 or slot_rows % 16:
        return False
    group = holders // matrices
    if group * chunk_width(columns, group) * 3 > columns * 4:
        return False
    return H % (BLOCKS * LANES) == 0 and H // 2 % (group * (shards // 2) * 16) == 0


def solution(mesh):
    def run(grad, momentum, lengths):
        matrices, slots, columns = grad.shape
        holders, shards = mesh.shape["dp"], mesh.shape["ep"]
        fits = can_split(holders, shards, matrices, slots // holders, columns // shards)
        return jax.shard_map(
            split_body if fits else gathered_body,
            mesh=mesh,
            in_specs=(P(None, "dp", "ep"), P(None, "dp", "ep"), P()),
            out_specs=(P(None, "dp", "ep"), P(None, "dp", "ep")),
            check_vma=False,
        )(grad, momentum, lengths)

    return run
```

```python
import functools
import math

import jax
import jax.numpy as jnp
from jax import lax
from jax.experimental import pallas as pl
from jax.experimental.pallas import tpu as pltpu
from jax.sharding import PartitionSpec as P

H = 1024
D = 3584


MOMENTUM_COEF = 0.95
EPSILON = 1e-06
FIRST_LIN = 3.0
FIRST_CUBE = -2.5
SECOND_LIN = 1.5
SECOND_CUBE = -0.5

LANES = 128
BLOCKS = 8
KEPT = BLOCKS // 2 + 1
MESH = pl.DeviceIdType.MESH
VMEM_LIMIT = 63 * 1024 * 1024


def from_root(block, axis, owner):
    block = jnp.where(lax.axis_index(axis) == owner, block, jnp.zeros_like(block))
    return lax.psum(block, axis)


def newton_polar(scaled_gram, factor, matrix):
    product = jnp.dot(scaled_gram, matrix, preferred_element_type=jnp.float32)
    first_iter = (factor * (FIRST_LIN * matrix.astype(jnp.float32) + FIRST_CUBE * product)).astype(
        jnp.bfloat16
    )
    product = jnp.dot(scaled_gram, first_iter, preferred_element_type=jnp.float32)
    applied = (FIRST_LIN * first_iter.astype(jnp.float32) + FIRST_CUBE * product).astype(
        jnp.bfloat16
    )
    second = jnp.dot(scaled_gram, applied, preferred_element_type=jnp.float32).astype(jnp.bfloat16)
    third = FIRST_LIN * second.astype(jnp.float32) + FIRST_CUBE * jnp.dot(
        scaled_gram, second, preferred_element_type=jnp.float32
    )
    return (SECOND_LIN * first_iter.astype(jnp.float32) + SECOND_CUBE * third).astype(jnp.bfloat16)


def gathered_body(grad, momentum, lengths):
    matrices = grad.shape[0]
    slot_rows = grad.shape[1]
    columns = grad.shape[2]
    new_momentum = MOMENTUM_COEF * momentum + grad
    rounded = (grad + MOMENTUM_COEF * new_momentum).astype(jnp.bfloat16)
    holders = lax.axis_size("dp")
    myself = lax.axis_index("dp")
    is_owner = myself < matrices
    chosen = jnp.minimum(myself, matrices - 1)
    offsets = jnp.cumsum(lengths, axis=1) - lengths
    chosen_len = lax.dynamic_index_in_dim(lengths, chosen, 0, keepdims=False)
    chosen_off = lax.dynamic_index_in_dim(offsets, chosen, 0, keepdims=False)
    device_ids = jnp.arange(holders, dtype=jnp.int32)
    portion = lax.all_gather(rounded, "dp", axis=1, tiled=True)
    piece_rows = portion.shape[1]
    incoming = lax.dynamic_index_in_dim(portion, chosen, 0, keepdims=False)
    slot_ids = jnp.arange(piece_rows, dtype=jnp.int32)
    source = slot_ids // slot_rows
    within = slot_ids % slot_rows
    matches = source[:, None] == device_ids[None, :]
    length_at = jnp.sum(jnp.where(matches, chosen_len[None, :], 0), axis=1)
    offset_at = jnp.sum(jnp.where(matches, chosen_off[None, :], 0), axis=1)
    keep = jnp.logical_and(within < length_at, is_owner)
    target = jnp.where(keep, offset_at + within, H)
    matrix = jnp.zeros((H, columns), jnp.bfloat16).at[target].set(incoming, mode="drop")
    portion = lax.all_gather(matrix, "ep", axis=1, tiled=True)
    gram_full = jnp.dot(portion, portion.T, preferred_element_type=jnp.float32)
    scale_sq = lax.rsqrt(jnp.sum(gram_full * gram_full) + EPSILON)
    scaled_gram = (scale_sq * gram_full).astype(jnp.bfloat16)
    ortho = newton_polar(scaled_gram, jnp.sqrt(scale_sq), matrix)
    scale_out = math.sqrt(max(H, D))
    positions = jnp.arange(slot_rows, dtype=jnp.int32)
    results = []
    for matrix_id in range(matrices):
        owned_ortho = from_root(ortho, "dp", matrix_id)
        own_length = lax.dynamic_index_in_dim(lengths[matrix_id], myself, 0, keepdims=False)
        own_offset = lax.dynamic_index_in_dim(offsets[matrix_id], myself, 0, keepdims=False)
        is_valid = positions < own_length
        picked = jnp.take(owned_ortho, jnp.where(is_valid, own_offset + positions, 0), axis=0)
        results.append(
            jnp.where(is_valid[:, None], picked.astype(jnp.float32) * scale_out, jnp.float32(0.0))
        )
    return (new_momentum, jnp.stack(results))


def other_core(ep):
    return ep + 1 - 2 * lax.rem(ep, 2)


def rows_at(index, count):
    return pl.ds(pl.multiple_of(index * count, count), count)


def step_kernel(
    holders,
    shards,
    lengths_ref,
    grad_hbm,
    momentum_hbm,
    back_ref,
    grad_ref,
    momentum_ref,
    rounded,
    held,
    packed,
    both,
    parts,
    terms,
    reduced,
    gram,
    first,
    applied,
    slots,
    chunk_sems,
    core_sems,
    term_sems,
    block_sems,
    half_sems,
    slot_sems,
    load_sems,
    local,
):
    matrices, slot_rows, columns = grad_ref.shape
    group = holders // matrices
    chips = shards // 2
    peers = group * chips
    width = held.shape[2]
    narrow = columns - (group - 1) * width
    height = both.shape[0]
    block = height // BLOCKS
    part_rows = height // 2 // peers
    span = KEPT * block

    dp, ep = lax.axis_index("dp"), lax.axis_index("ep")
    core = lax.rem(ep, 2)
    mine = dp // group
    place = lax.rem(dp, group)
    base = dp - place
    sibling = (dp, other_core(ep))

    def chunk_of(index, core):
        return lax.rem(index + core, group)

    def with_width(chunk, use):
        @pl.when(chunk < group - 1)
        def _():
            use(width)

        @pl.when(chunk == group - 1)
        def _():
            use(narrow)

    own_chunk = chunk_of(place, core)
    sibling_chunk = chunk_of(place, 1 - core)

    partners = [(lax.rem(dp + r, holders), ep) for r in range(1, holders)] + [sibling]
    for chip in range(1, chips):
        other = lax.rem(ep // 2 + chip, chips) * 2 + core
        partners += [(base + k, other) for k in range(group)]

    def load(j):
        return [
            pltpu.make_async_copy(source.at[j], target.at[j], load_sems.at[which, j])
            for which, (source, target) in enumerate(
                [(grad_hbm, grad_ref), (momentum_hbm, momentum_ref)]
            )
        ]

    for t in range(1, matrices + 1):
        for copy in load(lax.rem(mine + t, matrices)):
            copy.start()
    if narrow < width:
        held[:, :, narrow:] = jnp.zeros((2, held.shape[1], width - narrow), held.dtype)
    barrier = pltpu.get_barrier_semaphore()
    for partner in partners:
        pl.semaphore_signal(barrier, inc=1, device_id=partner, device_id_type=MESH)

    def round_rows(j):
        for copy in load(j):
            copy.wait()
        momentum = MOMENTUM_COEF * momentum_ref[j] + grad_ref[j]
        rounded[j] = (grad_ref[j] + MOMENTUM_COEF * momentum).astype(rounded.dtype)

    def chunk_copy(to, r, w):
        start = pl.multiple_of(chunk_of(lax.rem(to, group), core) * width, LANES)
        return pltpu.make_async_remote_copy(
            src_ref=rounded.at[to // group, :, pl.ds(start, w)],
            dst_ref=held.at[0, rows_at(dp, slot_rows), pl.ds(0, w)],
            send_sem=chunk_sems.at[0, r],
            recv_sem=chunk_sems.at[1, r],
            device_id=(to, ep),
            device_id_type=MESH,
        )

    def core_copy(source, r, w):
        return pltpu.make_async_remote_copy(
            src_ref=held.at[0, rows_at(source, slot_rows), pl.ds(0, w)],
            dst_ref=held.at[1, rows_at(source, slot_rows), pl.ds(0, w)],
            send_sem=core_sems.at[0, r],
            recv_sem=core_sems.at[1, r],
            device_id=sibling,
            device_id_type=MESH,
        )

    round_rows(lax.rem(mine + 1, matrices))
    pl.semaphore_wait(barrier, len(partners))
    order = []
    for t in range(1, matrices + 1):
        if t > 1:
            round_rows(lax.rem(mine + t, matrices))
        for k in range(group):
            if t == matrices and k == 0:
                continue
            order.append((t % matrices) * group + k)
            to = lax.rem(mine + t, matrices) * group + lax.rem(place + k, group)
            r = order[-1]
            chunk = chunk_of(lax.rem(to, group), core)
            with_width(chunk, lambda w, to=to, r=r: chunk_copy(to, r, w).start())

    def own_move(w):
        start = pl.multiple_of(own_chunk * width, LANES)
        move = pltpu.make_async_copy(
            rounded.at[mine, :, pl.ds(start, w)],
            held.at[0, rows_at(dp, slot_rows), pl.ds(0, w)],
            local,
        )
        move.start()
        move.wait()

    with_width(own_chunk, own_move)
    with_width(own_chunk, lambda w: core_copy(dp, 0, w).start())

    def source_of(r):
        t, k = r // group, r % group
        half = lax.rem(mine + matrices - t, matrices)
        return half * group + lax.rem(place + group - k, group)

    def first_row(holder):
        row = core * (height // 2)
        for d in range(holders):
            row = row + jnp.where(d < holder, lengths_ref[mine, d], 0)
        return row

    tile = 512
    half_slots = group * slot_rows

    def pack(half, open_sum, close_sum):
        slot = lax.broadcasted_iota(jnp.int32, (1, half_slots), 1)
        target = jnp.full((1, half_slots), -1, jnp.int32)
        for k in range(group):
            start = first_row(half * group + k)
            live = lengths_ref[mine, half * group + k]
            inside = jnp.logical_and(slot >= k * slot_rows, slot < k * slot_rows + live)
            row = slot - k * slot_rows + start
            target = jnp.where(inside, jnp.where(row >= height, row - height, row), target)

        def run(step, carry):
            start = pl.multiple_of(step * tile, tile)
            rows = lax.broadcasted_iota(jnp.int32, (tile, half_slots), 0) + start
            chosen = jnp.where(rows == target, 1.0, 0.0).astype(jnp.bfloat16)
            for which in range(2):
                at = pl.ds(start, tile), pl.ds(which * width, width)
                value = jnp.dot(
                    chosen,
                    held[which, rows_at(half, half_slots), :],
                    preferred_element_type=jnp.float32,
                )
                if not open_sum:
                    value = value + packed[at]
                if close_sum:
                    both[at] = value.astype(jnp.bfloat16)
                else:
                    packed[at] = value
            return carry

        lax.fori_loop(0, height // tile, run, 0)

    for t in range(matrices):
        arrivals = [r for r in order if r // group == t]
        for r in arrivals:

            def pass_on(w, r=r):
                chunk_copy(dp, r, w).wait_recv()
                core_copy(source_of(r), r, w).start()

            with_width(own_chunk, pass_on)
        for r in ([0] if t == 0 else []) + arrivals:
            with_width(sibling_chunk, lambda w, r=r: core_copy(dp, r, w).wait_recv())
        pack(lax.rem(mine + matrices - t, matrices), t == 0, t == matrices - 1)

    me = place * chips + ep // 2

    def device(index):
        return (base + index // chips, lax.rem(index, chips) * 2 + core)

    def term_copy(to, r):
        return pltpu.make_async_remote_copy(
            src_ref=parts.at[rows_at(to, part_rows)],
            dst_ref=terms.at[r],
            send_sem=term_sems.at[0, r],
            recv_sem=term_sems.at[1, r],
            device_id=device(to),
            device_id_type=MESH,
        )

    owners = block // part_rows
    for t in range(1, BLOCKS // 2 + 1):
        row = lax.rem(me // owners + t, BLOCKS // 2)
        start = pl.multiple_of(row * block, block)
        part = lax.dot_general(
            both[pl.ds(start, block), :],
            both[pl.ds(start, span), :],
            (((1,), (1,)), ((), ())),
            preferred_element_type=jnp.float32,
        )
        parts[pl.ds(start, block), :] = part.astype(jnp.bfloat16)
        for k in range(owners):
            if t == BLOCKS // 2 and k == 0:
                continue
            to = row * owners + lax.rem(me + k, owners)
            term_copy(to, lax.rem(to + peers - me, peers)).start()
    total = parts[rows_at(me, part_rows), :].astype(jnp.float32)
    for r in range(1, peers):
        term_copy(me, r).wait_recv()
        total = total + terms[r].astype(jnp.float32)
    reduced[...] = total.astype(reduced.dtype)

    def blocks_at(index, half):
        row = half * (height // 2) + index * part_rows
        column = pl.multiple_of(row // block * block, block)
        return gram.at[pl.ds(pl.multiple_of(row, part_rows), part_rows), pl.ds(column, span)]

    def block_copy(to, r):
        return pltpu.make_async_remote_copy(
            src_ref=reduced,
            dst_ref=blocks_at(me, 0),
            send_sem=block_sems.at[0, r],
            recv_sem=block_sems.at[1, r],
            device_id=device(to),
            device_id_type=MESH,
        )

    def half_copy(source, r):
        return pltpu.make_async_remote_copy(
            src_ref=reduced if r == 0 else blocks_at(source, 0),
            dst_ref=blocks_at(source, 1),
            send_sem=half_sems.at[0, r],
            recv_sem=half_sems.at[1, r],
            device_id=sibling,
            device_id_type=MESH,
        )

    for r in range(1, peers):
        block_copy(lax.rem(me + r, peers), r).start()
    half_copy(me, 0).start()
    own = pltpu.make_async_copy(reduced, blocks_at(me, 0), local)
    own.start()
    for r in range(1, peers):
        block_copy(me, r).wait_recv()
        half_copy(lax.rem(me + peers - r, peers), r).start()
    own.wait()

    squares = jnp.zeros((8, LANES), jnp.float32)
    for i in range(BLOCKS):
        if i == BLOCKS // 2:
            for r in range(peers):
                half_copy(me, r).wait_recv()
        for k in range(KEPT):
            j = (i + k) % BLOCKS
            piece = gram[pl.ds(i * block, block), pl.ds((i + k) * block, block)]
            if i + k >= BLOCKS:
                gram[pl.ds(i * block, block), pl.ds(j * block, block)] = piece
            wide = piece.astype(jnp.float32)
            twice = 0 < k < BLOCKS - KEPT + 1
            if twice:
                gram[pl.ds(j * block, block), pl.ds(i * block, block)] = piece.T
            square = (wide * wide).reshape(-1, 8, block).sum(axis=0)
            for lane in range(block // LANES):
                squares = squares + (2.0 if twice else 1.0) * square[
                    :, lane * LANES : (lane + 1) * LANES
                ]
    scale_sq = lax.rsqrt(jnp.sum(squares, keepdims=True) + EPSILON)
    factor = jnp.sqrt(scale_sq)

    def product(start, right):
        return scale_sq * jnp.dot(
            gram[pl.ds(start, tile), :height], right, preferred_element_type=jnp.float32
        )

    def each(step):
        def run(index, carry):
            step(pl.multiple_of(index * tile, tile))
            return carry

        lax.fori_loop(0, height // tile, run, 0)

    def one(start):
        rows = both[pl.ds(start, tile), :width].astype(jnp.float32)
        value = factor * (FIRST_LIN * rows + FIRST_CUBE * product(start, both[:, :width]))
        first[pl.ds(start, tile), :] = value.astype(jnp.bfloat16)

    def two(start):
        rows = first[pl.ds(start, tile), :].astype(jnp.float32)
        value = FIRST_LIN * rows + FIRST_CUBE * product(start, first[...])
        applied[0, pl.ds(start, tile), :] = value.astype(jnp.bfloat16)

    def three(start):
        value = product(start, applied[0])
        applied[1, pl.ds(start, tile), :] = value.astype(jnp.bfloat16)

    def four(start):
        rows = applied[1, pl.ds(start, tile), :].astype(jnp.float32)
        third = FIRST_LIN * rows + FIRST_CUBE * product(start, applied[1])
        rows = first[pl.ds(start, tile), :].astype(jnp.float32)
        value = SECOND_LIN * rows + SECOND_CUBE * third
        applied[0, pl.ds(start, tile), :] = value.astype(jnp.bfloat16)

    for step in (one, two, three, four):
        each(step)

    def slot_copy(to, r, w):
        start = pl.multiple_of(own_chunk * width, LANES)
        return pltpu.make_async_remote_copy(
            src_ref=slots.at[rows_at(to, slot_rows), pl.ds(0, w)],
            dst_ref=back_ref.at[mine, :, pl.ds(start, w)],
            send_sem=slot_sems.at[0, r],
            recv_sem=slot_sems.at[1, r],
            device_id=(to, ep),
            device_id_type=MESH,
        )

    def incoming(r, w):
        source = source_of(r)
        start = pl.multiple_of(chunk_of(lax.rem(source, group), core) * width, LANES)
        return pltpu.make_async_remote_copy(
            src_ref=slots.at[rows_at(source, slot_rows), pl.ds(0, w)],
            dst_ref=back_ref.at[source // group, :, pl.ds(start, w)],
            send_sem=slot_sems.at[0, r],
            recv_sem=slot_sems.at[1, r],
            device_id=(source, ep),
            device_id_type=MESH,
        )

    def lay_out(to):
        start = core * (height // 2)
        live = lengths_ref[mine, to]
        for d in range(holders):
            start = start + jnp.where(d < to, lengths_ref[mine, d], 0)
        slot = lax.broadcasted_iota(jnp.int32, (slot_rows, height), 0)
        column = lax.broadcasted_iota(jnp.int32, (slot_rows, height), 1)
        row = slot + start
        row = jnp.where(row >= height, row - height, row)
        row = jnp.where(row >= height, row - height, row)
        chosen = jnp.where(jnp.logical_and(row == column, slot < live), 1.0, 0.0)
        rows = jnp.dot(
            chosen.astype(jnp.bfloat16), applied[0], preferred_element_type=jnp.float32
        )
        slots[rows_at(to, slot_rows), :] = rows.astype(jnp.bfloat16)

    def target_of(r):
        t, k = r // group, r % group
        return lax.rem(mine + t, matrices) * group + lax.rem(place + k, group)

    for r in order:
        to = target_of(r)
        lay_out(to)
        with_width(own_chunk, lambda w, to=to, r=r: slot_copy(to, r, w).start())
    lay_out(dp)

    def keep(w):
        start = pl.multiple_of(own_chunk * width, LANES)
        move = pltpu.make_async_copy(
            slots.at[rows_at(dp, slot_rows), pl.ds(0, w)],
            back_ref.at[mine, :, pl.ds(start, w)],
            local,
        )
        move.start()
        move.wait()

    with_width(own_chunk, keep)

    for r in order:
        to = target_of(r)
        chunk = chunk_of(lax.rem(to, group), core)
        with_width(chunk, lambda w, to=to, r=r: chunk_copy(to, r, w).wait_send())
    for r in [0] + order:
        with_width(own_chunk, lambda w, r=r: core_copy(dp, r, w).wait_send())
    for r in range(1, peers):
        term_copy(me, r).wait_send()
        block_copy(me, r).wait_send()
    for r in range(peers):
        half_copy(me, r).wait_send()
    for r in order:
        with_width(own_chunk, lambda w, r=r: slot_copy(dp, r, w).wait_send())
        chunk = chunk_of(lax.rem(source_of(r), group), core)
        with_width(chunk, lambda w, r=r: incoming(r, w).wait_recv())


def orthogonalize(grad, momentum, lengths):
    matrices, slot_rows, columns = grad.shape
    holders, shards = lax.axis_size("dp"), lax.axis_size("ep")
    group = holders // matrices
    peers = group * (shards // 2)
    width = chunk_width(columns, group)
    block = H // BLOCKS
    part = (H // 2 // peers, KEPT * block)
    held = (2, holders * slot_rows, width)
    dma = pltpu.SemaphoreType.DMA
    hbm = pl.BlockSpec(memory_space=pl.ANY)

    def buffer(*shape):
        return pltpu.VMEM(shape, jnp.bfloat16)

    return pl.pallas_call(
        functools.partial(step_kernel, holders, shards),
        out_shape=jax.ShapeDtypeStruct(grad.shape, jnp.bfloat16),
        in_specs=[pl.BlockSpec(memory_space=pltpu.SMEM), hbm, hbm],
        out_specs=hbm,
        scratch_shapes=[
            pltpu.VMEM(grad.shape, jnp.float32),
            pltpu.VMEM(grad.shape, jnp.float32),
            buffer(*grad.shape),
            buffer(*held),
            pltpu.VMEM((H, 2 * width), jnp.float32),
            buffer(H, 2 * width),
            buffer(H // 2, KEPT * block),
            buffer(peers, *part),
            buffer(*part),
            buffer(H, H + (KEPT - 1) * block),
            buffer(H, width),
            buffer(2, H, width),
            buffer(holders * slot_rows, width),
            dma((2, holders)),
            dma((2, holders)),
            dma((2, peers)),
            dma((2, peers)),
            dma((2, peers)),
            dma((2, holders)),
            dma((2, matrices)),
            dma,
        ],
        compiler_params=pltpu.CompilerParams(
            collective_id=0, has_side_effects=True, vmem_limit_bytes=VMEM_LIMIT
        ),
        name="orthogonalize",
    )(lengths, grad, momentum)


def chunk_width(columns, group):
    return -(-columns // (group * LANES)) * LANES


def split_body(grad, momentum, lengths):
    new_momentum = MOMENTUM_COEF * momentum + grad
    back = orthogonalize(grad, momentum, lengths)
    return (new_momentum, back.astype(jnp.float32) * math.sqrt(max(H, D)))


def can_split(holders, shards, matrices, slot_rows, columns):
    if holders % matrices or shards % 2 or slot_rows % 16:
        return False
    group = holders // matrices
    if group * chunk_width(columns, group) * 3 > columns * 4:
        return False
    return H % (BLOCKS * LANES) == 0 and H // 2 % (group * (shards // 2) * 16) == 0


def solution(mesh):
    def run(grad, momentum, lengths):
        matrices, slots, columns = grad.shape
        holders, shards = mesh.shape["dp"], mesh.shape["ep"]
        fits = can_split(holders, shards, matrices, slots // holders, columns // shards)
        return jax.shard_map(
            split_body if fits else gathered_body,
            mesh=mesh,
            in_specs=(P(None, "dp", "ep"), P(None, "dp", "ep"), P()),
            out_specs=(P(None, "dp", "ep"), P(None, "dp", "ep")),
            check_vma=False,
        )(grad, momentum, lengths)

    return run
```

```python
import functools
import math

import jax
import jax.numpy as jnp
from jax import lax
from jax.experimental import pallas as pl
from jax.experimental.pallas import tpu as pltpu
from jax.sharding import PartitionSpec as P

H = 1024
D = 3584


MOMENTUM_COEF = 0.95
EPSILON = 1e-06
FIRST_LIN = 3.0
FIRST_CUBE = -2.5
SECOND_LIN = 1.5
SECOND_CUBE = -0.5

LANES = 128
BLOCKS = 8
KEPT = BLOCKS // 2 + 1
MESH = pl.DeviceIdType.MESH
VMEM_LIMIT = 58 * 1024 * 1024


def from_root(block, axis, owner):
    block = jnp.where(lax.axis_index(axis) == owner, block, jnp.zeros_like(block))
    return lax.psum(block, axis)


def newton_polar(scaled_gram, factor, matrix):
    product = jnp.dot(scaled_gram, matrix, preferred_element_type=jnp.float32)
    first_iter = (factor * (FIRST_LIN * matrix.astype(jnp.float32) + FIRST_CUBE * product)).astype(
        jnp.bfloat16
    )
    product = jnp.dot(scaled_gram, first_iter, preferred_element_type=jnp.float32)
    applied = (FIRST_LIN * first_iter.astype(jnp.float32) + FIRST_CUBE * product).astype(
        jnp.bfloat16
    )
    second = jnp.dot(scaled_gram, applied, preferred_element_type=jnp.float32).astype(jnp.bfloat16)
    third = FIRST_LIN * second.astype(jnp.float32) + FIRST_CUBE * jnp.dot(
        scaled_gram, second, preferred_element_type=jnp.float32
    )
    return (SECOND_LIN * first_iter.astype(jnp.float32) + SECOND_CUBE * third).astype(jnp.bfloat16)


def gathered_body(grad, momentum, lengths):
    matrices = grad.shape[0]
    slot_rows = grad.shape[1]
    columns = grad.shape[2]
    new_momentum = MOMENTUM_COEF * momentum + grad
    rounded = (grad + MOMENTUM_COEF * new_momentum).astype(jnp.bfloat16)
    holders = lax.axis_size("dp")
    myself = lax.axis_index("dp")
    is_owner = myself < matrices
    chosen = jnp.minimum(myself, matrices - 1)
    offsets = jnp.cumsum(lengths, axis=1) - lengths
    chosen_len = lax.dynamic_index_in_dim(lengths, chosen, 0, keepdims=False)
    chosen_off = lax.dynamic_index_in_dim(offsets, chosen, 0, keepdims=False)
    device_ids = jnp.arange(holders, dtype=jnp.int32)
    portion = lax.all_gather(rounded, "dp", axis=1, tiled=True)
    piece_rows = portion.shape[1]
    incoming = lax.dynamic_index_in_dim(portion, chosen, 0, keepdims=False)
    slot_ids = jnp.arange(piece_rows, dtype=jnp.int32)
    source = slot_ids // slot_rows
    within = slot_ids % slot_rows
    matches = source[:, None] == device_ids[None, :]
    length_at = jnp.sum(jnp.where(matches, chosen_len[None, :], 0), axis=1)
    offset_at = jnp.sum(jnp.where(matches, chosen_off[None, :], 0), axis=1)
    keep = jnp.logical_and(within < length_at, is_owner)
    target = jnp.where(keep, offset_at + within, H)
    matrix = jnp.zeros((H, columns), jnp.bfloat16).at[target].set(incoming, mode="drop")
    portion = lax.all_gather(matrix, "ep", axis=1, tiled=True)
    gram_full = jnp.dot(portion, portion.T, preferred_element_type=jnp.float32)
    scale_sq = lax.rsqrt(jnp.sum(gram_full * gram_full) + EPSILON)
    scaled_gram = (scale_sq * gram_full).astype(jnp.bfloat16)
    ortho = newton_polar(scaled_gram, jnp.sqrt(scale_sq), matrix)
    scale_out = math.sqrt(max(H, D))
    positions = jnp.arange(slot_rows, dtype=jnp.int32)
    results = []
    for matrix_id in range(matrices):
        owned_ortho = from_root(ortho, "dp", matrix_id)
        own_length = lax.dynamic_index_in_dim(lengths[matrix_id], myself, 0, keepdims=False)
        own_offset = lax.dynamic_index_in_dim(offsets[matrix_id], myself, 0, keepdims=False)
        is_valid = positions < own_length
        picked = jnp.take(owned_ortho, jnp.where(is_valid, own_offset + positions, 0), axis=0)
        results.append(
            jnp.where(is_valid[:, None], picked.astype(jnp.float32) * scale_out, jnp.float32(0.0))
        )
    return (new_momentum, jnp.stack(results))


def other_core(ep):
    return ep + 1 - 2 * lax.rem(ep, 2)


def rows_at(index, count):
    return pl.ds(pl.multiple_of(index * count, count), count)


def step_kernel(
    holders,
    shards,
    lengths_ref,
    grad_hbm,
    momentum_hbm,
    back_ref,
    fresh_ref,
    grad_ref,
    momentum_ref,
    rounded,
    held,
    packed,
    both,
    parts,
    terms,
    reduced,
    gram,
    first,
    applied,
    slots,
    chunk_sems,
    core_sems,
    term_sems,
    block_sems,
    half_sems,
    slot_sems,
    load_sems,
    local,
):
    matrices, slot_rows, columns = grad_ref.shape
    group = holders // matrices
    chips = shards // 2
    peers = group * chips
    width = held.shape[2]
    narrow = columns - (group - 1) * width
    height = both.shape[0]
    block = height // BLOCKS
    part_rows = height // 2 // peers
    span = KEPT * block

    dp, ep = lax.axis_index("dp"), lax.axis_index("ep")
    core = lax.rem(ep, 2)
    mine = dp // group
    place = lax.rem(dp, group)
    base = dp - place
    sibling = (dp, other_core(ep))

    def chunk_of(index, core):
        return lax.rem(index + core, group)

    def with_width(chunk, use):
        @pl.when(chunk < group - 1)
        def _():
            use(width)

        @pl.when(chunk == group - 1)
        def _():
            use(narrow)

    own_chunk = chunk_of(place, core)
    sibling_chunk = chunk_of(place, 1 - core)

    partners = [(lax.rem(dp + r, holders), ep) for r in range(1, holders)] + [sibling]
    for chip in range(1, chips):
        other = lax.rem(ep // 2 + chip, chips) * 2 + core
        partners += [(base + k, other) for k in range(group)]

    def load(j):
        return [
            pltpu.make_async_copy(source.at[j], target.at[j], load_sems.at[which, j])
            for which, (source, target) in enumerate(
                [(grad_hbm, grad_ref), (momentum_hbm, momentum_ref)]
            )
        ]

    for t in range(1, matrices + 1):
        for copy in load(lax.rem(mine + t, matrices)):
            copy.start()
    if narrow < width:
        held[:, :, narrow:] = jnp.zeros((2, held.shape[1], width - narrow), held.dtype)
    barrier = pltpu.get_barrier_semaphore()
    for partner in partners:
        pl.semaphore_signal(barrier, inc=1, device_id=partner, device_id_type=MESH)

    def round_rows(j):
        for copy in load(j):
            copy.wait()
        momentum = MOMENTUM_COEF * momentum_ref[j] + grad_ref[j]
        fresh_ref[j] = momentum
        rounded[j] = (grad_ref[j] + MOMENTUM_COEF * momentum).astype(rounded.dtype)

    def chunk_copy(to, r, w):
        start = pl.multiple_of(chunk_of(lax.rem(to, group), core) * width, LANES)
        return pltpu.make_async_remote_copy(
            src_ref=rounded.at[to // group, :, pl.ds(start, w)],
            dst_ref=held.at[0, rows_at(dp, slot_rows), pl.ds(0, w)],
            send_sem=chunk_sems.at[0, r],
            recv_sem=chunk_sems.at[1, r],
            device_id=(to, ep),
            device_id_type=MESH,
        )

    def core_copy(source, r, w):
        return pltpu.make_async_remote_copy(
            src_ref=held.at[0, rows_at(source, slot_rows), pl.ds(0, w)],
            dst_ref=held.at[1, rows_at(source, slot_rows), pl.ds(0, w)],
            send_sem=core_sems.at[0, r],
            recv_sem=core_sems.at[1, r],
            device_id=sibling,
            device_id_type=MESH,
        )

    round_rows(lax.rem(mine + 1, matrices))
    pl.semaphore_wait(barrier, len(partners))
    order = []
    for t in range(1, matrices + 1):
        if t > 1:
            round_rows(lax.rem(mine + t, matrices))
        for k in range(group):
            if t == matrices and k == 0:
                continue
            order.append((t % matrices) * group + k)
            to = lax.rem(mine + t, matrices) * group + lax.rem(place + k, group)
            r = order[-1]
            chunk = chunk_of(lax.rem(to, group), core)
            with_width(chunk, lambda w, to=to, r=r: chunk_copy(to, r, w).start())

    def own_move(w):
        start = pl.multiple_of(own_chunk * width, LANES)
        move = pltpu.make_async_copy(
            rounded.at[mine, :, pl.ds(start, w)],
            held.at[0, rows_at(dp, slot_rows), pl.ds(0, w)],
            local,
        )
        move.start()
        move.wait()

    with_width(own_chunk, own_move)
    with_width(own_chunk, lambda w: core_copy(dp, 0, w).start())

    def source_of(r):
        t, k = r // group, r % group
        half = lax.rem(mine + matrices - t, matrices)
        return half * group + lax.rem(place + group - k, group)

    def first_row(holder):
        row = core * (height // 2)
        for d in range(holders):
            row = row + jnp.where(d < holder, lengths_ref[mine, d], 0)
        return row

    tile = 512
    half_slots = group * slot_rows

    def pack(half, open_sum, close_sum):
        slot = lax.broadcasted_iota(jnp.int32, (1, half_slots), 1)
        target = jnp.full((1, half_slots), -1, jnp.int32)
        for k in range(group):
            start = first_row(half * group + k)
            live = lengths_ref[mine, half * group + k]
            inside = jnp.logical_and(slot >= k * slot_rows, slot < k * slot_rows + live)
            row = slot - k * slot_rows + start
            target = jnp.where(inside, jnp.where(row >= height, row - height, row), target)

        def run(step, carry):
            start = pl.multiple_of(step * tile, tile)
            rows = lax.broadcasted_iota(jnp.int32, (tile, half_slots), 0) + start
            chosen = jnp.where(rows == target, 1.0, 0.0).astype(jnp.bfloat16)
            for which in range(2):
                at = pl.ds(start, tile), pl.ds(which * width, width)
                value = jnp.dot(
                    chosen,
                    held[which, rows_at(half, half_slots), :],
                    preferred_element_type=jnp.float32,
                )
                if not open_sum:
                    value = value + packed[at]
                if close_sum:
                    both[at] = value.astype(jnp.bfloat16)
                else:
                    packed[at] = value
            return carry

        lax.fori_loop(0, height // tile, run, 0)

    for t in range(matrices):
        arrivals = [r for r in order if r // group == t]
        for r in arrivals:

            def pass_on(w, r=r):
                chunk_copy(dp, r, w).wait_recv()
                core_copy(source_of(r), r, w).start()

            with_width(own_chunk, pass_on)
        for r in ([0] if t == 0 else []) + arrivals:
            with_width(sibling_chunk, lambda w, r=r: core_copy(dp, r, w).wait_recv())
        pack(lax.rem(mine + matrices - t, matrices), t == 0, t == matrices - 1)

    me = place * chips + ep // 2

    def device(index):
        return (base + index // chips, lax.rem(index, chips) * 2 + core)

    def term_copy(to, r):
        return pltpu.make_async_remote_copy(
            src_ref=parts.at[rows_at(to, part_rows)],
            dst_ref=terms.at[r],
            send_sem=term_sems.at[0, r],
            recv_sem=term_sems.at[1, r],
            device_id=device(to),
            device_id_type=MESH,
        )

    owners = block // part_rows
    for t in range(1, BLOCKS // 2 + 1):
        row = lax.rem(me // owners + t, BLOCKS // 2)
        start = pl.multiple_of(row * block, block)
        part = lax.dot_general(
            both[pl.ds(start, block), :],
            both[pl.ds(start, span), :],
            (((1,), (1,)), ((), ())),
            preferred_element_type=jnp.float32,
        )
        parts[pl.ds(start, block), :] = part.astype(jnp.bfloat16)
        for k in range(owners):
            if t == BLOCKS // 2 and k == 0:
                continue
            to = row * owners + lax.rem(me + k, owners)
            term_copy(to, lax.rem(to + peers - me, peers)).start()
    total = parts[rows_at(me, part_rows), :].astype(jnp.float32)
    for r in range(1, peers):
        term_copy(me, r).wait_recv()
        total = total + terms[r].astype(jnp.float32)
    reduced[...] = total.astype(reduced.dtype)

    def blocks_at(index, half):
        row = half * (height // 2) + index * part_rows
        column = pl.multiple_of(row // block * block, block)
        return gram.at[pl.ds(pl.multiple_of(row, part_rows), part_rows), pl.ds(column, span)]

    def block_copy(to, r):
        return pltpu.make_async_remote_copy(
            src_ref=reduced,
            dst_ref=blocks_at(me, 0),
            send_sem=block_sems.at[0, r],
            recv_sem=block_sems.at[1, r],
            device_id=device(to),
            device_id_type=MESH,
        )

    def half_copy(source, r):
        return pltpu.make_async_remote_copy(
            src_ref=reduced if r == 0 else blocks_at(source, 0),
            dst_ref=blocks_at(source, 1),
            send_sem=half_sems.at[0, r],
            recv_sem=half_sems.at[1, r],
            device_id=sibling,
            device_id_type=MESH,
        )

    for r in range(1, peers):
        block_copy(lax.rem(me + r, peers), r).start()
    half_copy(me, 0).start()
    own = pltpu.make_async_copy(reduced, blocks_at(me, 0), local)
    own.start()
    for r in range(1, peers):
        block_copy(me, r).wait_recv()
        half_copy(lax.rem(me + peers - r, peers), r).start()
    own.wait()

    squares = jnp.zeros((8, LANES), jnp.float32)
    for i in range(BLOCKS):
        if i == BLOCKS // 2:
            for r in range(peers):
                half_copy(me, r).wait_recv()
        for k in range(KEPT):
            j = (i + k) % BLOCKS
            piece = gram[pl.ds(i * block, block), pl.ds((i + k) * block, block)]
            if i + k >= BLOCKS:
                gram[pl.ds(i * block, block), pl.ds(j * block, block)] = piece
            wide = piece.astype(jnp.float32)
            twice = 0 < k < BLOCKS - KEPT + 1
            if twice:
                gram[pl.ds(j * block, block), pl.ds(i * block, block)] = piece.T
            square = (wide * wide).reshape(-1, 8, block).sum(axis=0)
            for lane in range(block // LANES):
                squares = squares + (2.0 if twice else 1.0) * square[
                    :, lane * LANES : (lane + 1) * LANES
                ]
    scale_sq = lax.rsqrt(jnp.sum(squares, keepdims=True) + EPSILON)
    factor = jnp.sqrt(scale_sq)

    def product(start, right):
        return scale_sq * jnp.dot(
            gram[pl.ds(start, tile), :height], right, preferred_element_type=jnp.float32
        )

    def each(step):
        def run(index, carry):
            step(pl.multiple_of(index * tile, tile))
            return carry

        lax.fori_loop(0, height // tile, run, 0)

    def one(start):
        rows = both[pl.ds(start, tile), :width].astype(jnp.float32)
        value = factor * (FIRST_LIN * rows + FIRST_CUBE * product(start, both[:, :width]))
        first[pl.ds(start, tile), :] = value.astype(jnp.bfloat16)

    def two(start):
        rows = first[pl.ds(start, tile), :].astype(jnp.float32)
        value = FIRST_LIN * rows + FIRST_CUBE * product(start, first[...])
        applied[0, pl.ds(start, tile), :] = value.astype(jnp.bfloat16)

    def three(start):
        value = product(start, applied[0])
        applied[1, pl.ds(start, tile), :] = value.astype(jnp.bfloat16)

    def four(start):
        rows = applied[1, pl.ds(start, tile), :].astype(jnp.float32)
        third = FIRST_LIN * rows + FIRST_CUBE * product(start, applied[1])
        rows = first[pl.ds(start, tile), :].astype(jnp.float32)
        value = SECOND_LIN * rows + SECOND_CUBE * third
        applied[0, pl.ds(start, tile), :] = value.astype(jnp.bfloat16)

    for step in (one, two, three, four):
        each(step)

    def slot_copy(to, r, w):
        start = pl.multiple_of(own_chunk * width, LANES)
        return pltpu.make_async_remote_copy(
            src_ref=slots.at[rows_at(to, slot_rows), pl.ds(0, w)],
            dst_ref=back_ref.at[mine, :, pl.ds(start, w)],
            send_sem=slot_sems.at[0, r],
            recv_sem=slot_sems.at[1, r],
            device_id=(to, ep),
            device_id_type=MESH,
        )

    def incoming(r, w):
        source = source_of(r)
        start = pl.multiple_of(chunk_of(lax.rem(source, group), core) * width, LANES)
        return pltpu.make_async_remote_copy(
            src_ref=slots.at[rows_at(source, slot_rows), pl.ds(0, w)],
            dst_ref=back_ref.at[source // group, :, pl.ds(start, w)],
            send_sem=slot_sems.at[0, r],
            recv_sem=slot_sems.at[1, r],
            device_id=(source, ep),
            device_id_type=MESH,
        )

    def lay_out(to):
        start = core * (height // 2)
        live = lengths_ref[mine, to]
        for d in range(holders):
            start = start + jnp.where(d < to, lengths_ref[mine, d], 0)
        slot = lax.broadcasted_iota(jnp.int32, (slot_rows, height), 0)
        column = lax.broadcasted_iota(jnp.int32, (slot_rows, height), 1)
        row = slot + start
        row = jnp.where(row >= height, row - height, row)
        row = jnp.where(row >= height, row - height, row)
        chosen = jnp.where(jnp.logical_and(row == column, slot < live), 1.0, 0.0)
        rows = jnp.dot(
            chosen.astype(jnp.bfloat16), applied[0], preferred_element_type=jnp.float32
        )
        slots[rows_at(to, slot_rows), :] = rows.astype(jnp.bfloat16)

    def target_of(r):
        t, k = r // group, r % group
        return lax.rem(mine + t, matrices) * group + lax.rem(place + k, group)

    for r in order:
        to = target_of(r)
        lay_out(to)
        with_width(own_chunk, lambda w, to=to, r=r: slot_copy(to, r, w).start())
    lay_out(dp)

    def keep(w):
        start = pl.multiple_of(own_chunk * width, LANES)
        move = pltpu.make_async_copy(
            slots.at[rows_at(dp, slot_rows), pl.ds(0, w)],
            back_ref.at[mine, :, pl.ds(start, w)],
            local,
        )
        move.start()
        move.wait()

    with_width(own_chunk, keep)

    for r in order:
        to = target_of(r)
        chunk = chunk_of(lax.rem(to, group), core)
        with_width(chunk, lambda w, to=to, r=r: chunk_copy(to, r, w).wait_send())
    for r in [0] + order:
        with_width(own_chunk, lambda w, r=r: core_copy(dp, r, w).wait_send())
    for r in range(1, peers):
        term_copy(me, r).wait_send()
        block_copy(me, r).wait_send()
    for r in range(peers):
        half_copy(me, r).wait_send()
    for r in order:
        with_width(own_chunk, lambda w, r=r: slot_copy(dp, r, w).wait_send())
        chunk = chunk_of(lax.rem(source_of(r), group), core)
        with_width(chunk, lambda w, r=r: incoming(r, w).wait_recv())


def orthogonalize(grad, momentum, lengths):
    matrices, slot_rows, columns = grad.shape
    holders, shards = lax.axis_size("dp"), lax.axis_size("ep")
    group = holders // matrices
    peers = group * (shards // 2)
    width = chunk_width(columns, group)
    block = H // BLOCKS
    part = (H // 2 // peers, KEPT * block)
    held = (2, holders * slot_rows, width)
    dma = pltpu.SemaphoreType.DMA
    hbm = pl.BlockSpec(memory_space=pl.ANY)
    vmem = pl.BlockSpec(memory_space=pltpu.VMEM)

    def buffer(*shape):
        return pltpu.VMEM(shape, jnp.bfloat16)

    return pl.pallas_call(
        functools.partial(step_kernel, holders, shards),
        out_shape=(
            pltpu.VMEM(grad.shape, jnp.bfloat16),
            pltpu.VMEM(grad.shape, jnp.float32),
        ),
        in_specs=[pl.BlockSpec(memory_space=pltpu.SMEM), hbm, hbm],
        out_specs=(vmem, vmem),
        scratch_shapes=[
            pltpu.VMEM(grad.shape, jnp.float32),
            pltpu.VMEM(grad.shape, jnp.float32),
            buffer(*grad.shape),
            buffer(*held),
            pltpu.VMEM((H, 2 * width), jnp.float32),
            buffer(H, 2 * width),
            buffer(H // 2, KEPT * block),
            buffer(peers, *part),
            buffer(*part),
            buffer(H, H + (KEPT - 1) * block),
            buffer(H, width),
            buffer(2, H, width),
            buffer(holders * slot_rows, width),
            dma((2, holders)),
            dma((2, holders)),
            dma((2, peers)),
            dma((2, peers)),
            dma((2, peers)),
            dma((2, holders)),
            dma((2, matrices)),
            dma,
        ],
        compiler_params=pltpu.CompilerParams(
            collective_id=0, has_side_effects=True, vmem_limit_bytes=VMEM_LIMIT
        ),
        name="orthogonalize",
    )(lengths, grad, momentum)


def chunk_width(columns, group):
    return -(-columns // (group * LANES)) * LANES


def split_body(grad, momentum, lengths):
    back, new_momentum = orthogonalize(grad, momentum, lengths)
    return (new_momentum, back.astype(jnp.float32) * math.sqrt(max(H, D)))


def can_split(holders, shards, matrices, slot_rows, columns):
    if holders % matrices or shards % 2 or slot_rows % 16:
        return False
    group = holders // matrices
    if group * chunk_width(columns, group) * 3 > columns * 4:
        return False
    return H % (BLOCKS * LANES) == 0 and H // 2 % (group * (shards // 2) * 16) == 0


def solution(mesh):
    def run(grad, momentum, lengths):
        matrices, slots, columns = grad.shape
        holders, shards = mesh.shape["dp"], mesh.shape["ep"]
        fits = can_split(holders, shards, matrices, slots // holders, columns // shards)
        return jax.shard_map(
            split_body if fits else gathered_body,
            mesh=mesh,
            in_specs=(P(None, "dp", "ep"), P(None, "dp", "ep"), P()),
            out_specs=(P(None, "dp", "ep"), P(None, "dp", "ep")),
            check_vma=False,
        )(grad, momentum, lengths)

    return run
```

```python
import functools
import math

import jax
import jax.numpy as jnp
from jax import lax
from jax.experimental import pallas as pl
from jax.experimental.pallas import tpu as pltpu
from jax.sharding import PartitionSpec as P

H = 1024
D = 3584


MOMENTUM_COEF = 0.95
EPSILON = 1e-06
FIRST_LIN = 3.0
FIRST_CUBE = -2.5
SECOND_LIN = 1.5
SECOND_CUBE = -0.5

LANES = 128
BLOCKS = 8
KEPT = BLOCKS // 2 + 1
MESH = pl.DeviceIdType.MESH
VMEM_LIMIT = 58 * 1024 * 1024


def from_root(block, axis, owner):
    block = jnp.where(lax.axis_index(axis) == owner, block, jnp.zeros_like(block))
    return lax.psum(block, axis)


def newton_polar(scaled_gram, factor, matrix):
    product = jnp.dot(scaled_gram, matrix, preferred_element_type=jnp.float32)
    first_iter = (factor * (FIRST_LIN * matrix.astype(jnp.float32) + FIRST_CUBE * product)).astype(
        jnp.bfloat16
    )
    product = jnp.dot(scaled_gram, first_iter, preferred_element_type=jnp.float32)
    applied = (FIRST_LIN * first_iter.astype(jnp.float32) + FIRST_CUBE * product).astype(
        jnp.bfloat16
    )
    second = jnp.dot(scaled_gram, applied, preferred_element_type=jnp.float32).astype(jnp.bfloat16)
    third = FIRST_LIN * second.astype(jnp.float32) + FIRST_CUBE * jnp.dot(
        scaled_gram, second, preferred_element_type=jnp.float32
    )
    return (SECOND_LIN * first_iter.astype(jnp.float32) + SECOND_CUBE * third).astype(jnp.bfloat16)


def gathered_body(grad, momentum, lengths):
    matrices = grad.shape[0]
    slot_rows = grad.shape[1]
    columns = grad.shape[2]
    new_momentum = MOMENTUM_COEF * momentum + grad
    rounded = (grad + MOMENTUM_COEF * new_momentum).astype(jnp.bfloat16)
    holders = lax.axis_size("dp")
    myself = lax.axis_index("dp")
    is_owner = myself < matrices
    chosen = jnp.minimum(myself, matrices - 1)
    offsets = jnp.cumsum(lengths, axis=1) - lengths
    chosen_len = lax.dynamic_index_in_dim(lengths, chosen, 0, keepdims=False)
    chosen_off = lax.dynamic_index_in_dim(offsets, chosen, 0, keepdims=False)
    device_ids = jnp.arange(holders, dtype=jnp.int32)
    portion = lax.all_gather(rounded, "dp", axis=1, tiled=True)
    piece_rows = portion.shape[1]
    incoming = lax.dynamic_index_in_dim(portion, chosen, 0, keepdims=False)
    slot_ids = jnp.arange(piece_rows, dtype=jnp.int32)
    source = slot_ids // slot_rows
    within = slot_ids % slot_rows
    matches = source[:, None] == device_ids[None, :]
    length_at = jnp.sum(jnp.where(matches, chosen_len[None, :], 0), axis=1)
    offset_at = jnp.sum(jnp.where(matches, chosen_off[None, :], 0), axis=1)
    keep = jnp.logical_and(within < length_at, is_owner)
    target = jnp.where(keep, offset_at + within, H)
    matrix = jnp.zeros((H, columns), jnp.bfloat16).at[target].set(incoming, mode="drop")
    portion = lax.all_gather(matrix, "ep", axis=1, tiled=True)
    gram_full = jnp.dot(portion, portion.T, preferred_element_type=jnp.float32)
    scale_sq = lax.rsqrt(jnp.sum(gram_full * gram_full) + EPSILON)
    scaled_gram = (scale_sq * gram_full).astype(jnp.bfloat16)
    ortho = newton_polar(scaled_gram, jnp.sqrt(scale_sq), matrix)
    scale_out = math.sqrt(max(H, D))
    positions = jnp.arange(slot_rows, dtype=jnp.int32)
    results = []
    for matrix_id in range(matrices):
        owned_ortho = from_root(ortho, "dp", matrix_id)
        own_length = lax.dynamic_index_in_dim(lengths[matrix_id], myself, 0, keepdims=False)
        own_offset = lax.dynamic_index_in_dim(offsets[matrix_id], myself, 0, keepdims=False)
        is_valid = positions < own_length
        picked = jnp.take(owned_ortho, jnp.where(is_valid, own_offset + positions, 0), axis=0)
        results.append(
            jnp.where(is_valid[:, None], picked.astype(jnp.float32) * scale_out, jnp.float32(0.0))
        )
    return (new_momentum, jnp.stack(results))


def other_core(ep):
    return ep + 1 - 2 * lax.rem(ep, 2)


def rows_at(index, count):
    return pl.ds(pl.multiple_of(index * count, count), count)


def step_kernel(
    holders,
    shards,
    lengths_ref,
    grad_hbm,
    momentum_hbm,
    back_ref,
    fresh_ref,
    grad_ref,
    momentum_ref,
    rounded,
    held,
    packed,
    both,
    parts,
    terms,
    reduced,
    gram,
    squares,
    first,
    applied,
    slots,
    chunk_sems,
    core_sems,
    term_sems,
    block_sems,
    half_sems,
    own_sems,
    slot_sems,
    load_sems,
    local,
):
    matrices, slot_rows, columns = grad_ref.shape
    group = holders // matrices
    chips = shards // 2
    peers = group * chips
    width = held.shape[2]
    narrow = columns - (group - 1) * width
    height = both.shape[0]
    block = height // BLOCKS
    part_rows = height // 2 // peers
    span = KEPT * block

    dp, ep = lax.axis_index("dp"), lax.axis_index("ep")
    core = lax.rem(ep, 2)
    mine = dp // group
    place = lax.rem(dp, group)
    base = dp - place
    sibling = (dp, other_core(ep))

    def chunk_of(index, core):
        return lax.rem(index + core, group)

    def with_width(chunk, use):
        @pl.when(chunk < group - 1)
        def _():
            use(width)

        @pl.when(chunk == group - 1)
        def _():
            use(narrow)

    own_chunk = chunk_of(place, core)
    sibling_chunk = chunk_of(place, 1 - core)

    partners = [(lax.rem(dp + r, holders), ep) for r in range(1, holders)] + [sibling]
    for chip in range(1, chips):
        other = lax.rem(ep // 2 + chip, chips) * 2 + core
        partners += [(base + k, other) for k in range(group)]

    def load(j):
        return [
            pltpu.make_async_copy(source.at[j], target.at[j], load_sems.at[which, j])
            for which, (source, target) in enumerate(
                [(grad_hbm, grad_ref), (momentum_hbm, momentum_ref)]
            )
        ]

    for t in range(1, matrices + 1):
        for copy in load(lax.rem(mine + t, matrices)):
            copy.start()
    if narrow < width:
        held[:, :, narrow:] = jnp.zeros((2, held.shape[1], width - narrow), held.dtype)
    barrier = pltpu.get_barrier_semaphore()
    for partner in partners:
        pl.semaphore_signal(barrier, inc=1, device_id=partner, device_id_type=MESH)

    def round_rows(j):
        for copy in load(j):
            copy.wait()
        momentum = MOMENTUM_COEF * momentum_ref[j] + grad_ref[j]
        fresh_ref[j] = momentum
        rounded[j] = (grad_ref[j] + MOMENTUM_COEF * momentum).astype(rounded.dtype)

    def chunk_copy(to, r, w):
        start = pl.multiple_of(chunk_of(lax.rem(to, group), core) * width, LANES)
        return pltpu.make_async_remote_copy(
            src_ref=rounded.at[to // group, :, pl.ds(start, w)],
            dst_ref=held.at[0, rows_at(dp, slot_rows), pl.ds(0, w)],
            send_sem=chunk_sems.at[0, r],
            recv_sem=chunk_sems.at[1, r],
            device_id=(to, ep),
            device_id_type=MESH,
        )

    def core_copy(source, r, w):
        return pltpu.make_async_remote_copy(
            src_ref=held.at[0, rows_at(source, slot_rows), pl.ds(0, w)],
            dst_ref=held.at[1, rows_at(source, slot_rows), pl.ds(0, w)],
            send_sem=core_sems.at[0, r],
            recv_sem=core_sems.at[1, r],
            device_id=sibling,
            device_id_type=MESH,
        )

    round_rows(lax.rem(mine + 1, matrices))
    pl.semaphore_wait(barrier, len(partners))
    order = []
    for t in range(1, matrices + 1):
        if t > 1:
            round_rows(lax.rem(mine + t, matrices))
        for k in range(group):
            if t == matrices and k == 0:
                continue
            order.append((t % matrices) * group + k)
            to = lax.rem(mine + t, matrices) * group + lax.rem(place + k, group)
            r = order[-1]
            chunk = chunk_of(lax.rem(to, group), core)
            with_width(chunk, lambda w, to=to, r=r: chunk_copy(to, r, w).start())

    def own_move(w):
        start = pl.multiple_of(own_chunk * width, LANES)
        move = pltpu.make_async_copy(
            rounded.at[mine, :, pl.ds(start, w)],
            held.at[0, rows_at(dp, slot_rows), pl.ds(0, w)],
            local,
        )
        move.start()
        move.wait()

    with_width(own_chunk, own_move)
    with_width(own_chunk, lambda w: core_copy(dp, 0, w).start())

    def source_of(r):
        t, k = r // group, r % group
        half = lax.rem(mine + matrices - t, matrices)
        return half * group + lax.rem(place + group - k, group)

    def first_row(holder):
        row = core * (height // 2)
        for d in range(holders):
            row = row + jnp.where(d < holder, lengths_ref[mine, d], 0)
        return row

    tile = 512
    half_slots = group * slot_rows

    def pack(half, open_sum, close_sum):
        slot = lax.broadcasted_iota(jnp.int32, (1, half_slots), 1)
        target = jnp.full((1, half_slots), -1, jnp.int32)
        for k in range(group):
            start = first_row(half * group + k)
            live = lengths_ref[mine, half * group + k]
            inside = jnp.logical_and(slot >= k * slot_rows, slot < k * slot_rows + live)
            row = slot - k * slot_rows + start
            target = jnp.where(inside, jnp.where(row >= height, row - height, row), target)

        def run(step, carry):
            start = pl.multiple_of(step * tile, tile)
            rows = lax.broadcasted_iota(jnp.int32, (tile, half_slots), 0) + start
            chosen = jnp.where(rows == target, 1.0, 0.0).astype(jnp.bfloat16)
            for which in range(2):
                at = pl.ds(start, tile), pl.ds(which * width, width)
                value = jnp.dot(
                    chosen,
                    held[which, rows_at(half, half_slots), :],
                    preferred_element_type=jnp.float32,
                )
                if not open_sum:
                    value = value + packed[at]
                if close_sum:
                    both[at] = value.astype(jnp.bfloat16)
                else:
                    packed[at] = value
            return carry

        lax.fori_loop(0, height // tile, run, 0)

    for t in range(matrices):
        arrivals = [r for r in order if r // group == t]
        for r in arrivals:

            def pass_on(w, r=r):
                chunk_copy(dp, r, w).wait_recv()
                core_copy(source_of(r), r, w).start()

            with_width(own_chunk, pass_on)
        for r in ([0] if t == 0 else []) + arrivals:
            with_width(sibling_chunk, lambda w, r=r: core_copy(dp, r, w).wait_recv())
        pack(lax.rem(mine + matrices - t, matrices), t == 0, t == matrices - 1)

    me = place * chips + ep // 2

    def device(index):
        return (base + index // chips, lax.rem(index, chips) * 2 + core)

    split = 2 * block

    def with_span(piece, of_core, use):
        if piece == 0:
            use(split)
            return

        @pl.when(of_core == 0)
        def _():
            use(span - split)

        @pl.when(of_core != 0)
        def _():
            use(span - block - split)

    def term_copy(to, r, piece, w):
        return pltpu.make_async_remote_copy(
            src_ref=parts.at[rows_at(to, part_rows), pl.ds(piece * split, w)],
            dst_ref=terms.at[r, :, pl.ds(piece * split, w)],
            send_sem=term_sems.at[0, piece, r],
            recv_sem=term_sems.at[1, piece, r],
            device_id=device(to),
            device_id_type=MESH,
        )

    owners = block // part_rows
    for t in range(1, BLOCKS // 2 + 1):
        row = lax.rem(me // owners + t, BLOCKS // 2)
        start = pl.multiple_of(row * block, block)
        part = lax.dot_general(
            both[pl.ds(start, block), :],
            both[pl.ds(start, span), :],
            (((1,), (1,)), ((), ())),
            preferred_element_type=jnp.float32,
        )
        parts[pl.ds(start, block), :] = part.astype(jnp.bfloat16)
        for k in range(owners):
            if t == BLOCKS // 2 and k == 0:
                continue
            to = row * owners + lax.rem(me + k, owners)
            term_copy(to, lax.rem(to + peers - me, peers), 0, split).start()
    for r in range(1, peers):
        to = lax.rem(me + r, peers)
        with_span(1, core, lambda w, to=to, r=r: term_copy(to, r, 1, w).start())

    def blocks_at(index, half, piece, w):
        row = half * (height // 2) + index * part_rows
        column = pl.multiple_of(row // block * block, block) + piece * split
        return gram.at[
            pl.ds(pl.multiple_of(row, part_rows), part_rows),
            pl.ds(pl.multiple_of(column, block), w),
        ]

    def block_copy(to, r, piece, w):
        return pltpu.make_async_remote_copy(
            src_ref=reduced.at[:, pl.ds(piece * split, w)],
            dst_ref=blocks_at(me, 0, piece, w),
            send_sem=block_sems.at[0, piece, r],
            recv_sem=block_sems.at[1, piece, r],
            device_id=device(to),
            device_id_type=MESH,
        )

    def half_copy(source, r, piece, w):
        own = reduced.at[:, pl.ds(piece * split, w)]
        return pltpu.make_async_remote_copy(
            src_ref=own if r == 0 else blocks_at(source, 0, piece, w),
            dst_ref=blocks_at(source, 1, piece, w),
            send_sem=half_sems.at[0, piece, r],
            recv_sem=half_sems.at[1, piece, r],
            device_id=sibling,
            device_id_type=MESH,
        )

    def own_copy(piece, w):
        return pltpu.make_async_copy(
            reduced.at[:, pl.ds(piece * split, w)], blocks_at(me, 0, piece, w), own_sems.at[piece]
        )

    def reduce_piece(piece, w):
        at = pl.ds(piece * split, w)
        total = parts[rows_at(me, part_rows), at].astype(jnp.float32)
        for r in range(1, peers):
            term_copy(me, r, piece, w).wait_recv()
            total = total + terms[r, :, at].astype(jnp.float32)
        reduced[:, at] = total.astype(reduced.dtype)
        for r in range(1, peers):
            block_copy(lax.rem(me + r, peers), r, piece, w).start()
        half_copy(me, 0, piece, w).start()
        own_copy(piece, w).start()

    def forward_piece(piece, w):
        for r in range(1, peers):
            block_copy(me, r, piece, w).wait_recv()
            half_copy(lax.rem(me + peers - r, peers), r, piece, w).start()
        own_copy(piece, w).wait()

    def await_half(piece, w):
        for r in range(peers):
            half_copy(me, r, piece, w).wait_recv()

    def assemble(half, blocks):
        for i in range(half * BLOCKS // 2, (half + 1) * BLOCKS // 2):
            for k in blocks:

                def place(i=i, k=k):
                    j = (i + k) % BLOCKS
                    piece = gram[pl.ds(i * block, block), pl.ds((i + k) * block, block)]
                    if i + k >= BLOCKS:
                        gram[pl.ds(i * block, block), pl.ds(j * block, block)] = piece
                    if k > 0:
                        gram[pl.ds(j * block, block), pl.ds(i * block, block)] = piece.T
                    wide = piece.astype(jnp.float32)
                    square = (wide * wide).reshape(-1, 8, block).sum(axis=0)
                    squares[...] += (2.0 if k > 0 else 1.0) * square

                if k == KEPT - 1:
                    pl.when(core == half)(place)
                else:
                    place()

    squares[...] = jnp.zeros(squares.shape, squares.dtype)
    for piece in range(2):
        with_span(piece, core, functools.partial(reduce_piece, piece))
    for piece, blocks in ((0, range(2)), (1, range(2, KEPT))):
        with_span(piece, core, functools.partial(forward_piece, piece))
        assemble(0, blocks)
        with_span(piece, 1 - core, functools.partial(await_half, piece))
        assemble(1, blocks)
    scale_sq = lax.rsqrt(jnp.sum(squares[...], keepdims=True) + EPSILON)
    factor = jnp.sqrt(scale_sq)

    def product(start, right):
        return scale_sq * jnp.dot(
            gram[pl.ds(start, tile), :height], right, preferred_element_type=jnp.float32
        )

    def each(step):
        def run(index, carry):
            step(pl.multiple_of(index * tile, tile))
            return carry

        lax.fori_loop(0, height // tile, run, 0)

    def one(start):
        rows = both[pl.ds(start, tile), :width].astype(jnp.float32)
        value = factor * (FIRST_LIN * rows + FIRST_CUBE * product(start, both[:, :width]))
        first[pl.ds(start, tile), :] = value.astype(jnp.bfloat16)

    def two(start):
        rows = first[pl.ds(start, tile), :].astype(jnp.float32)
        value = FIRST_LIN * rows + FIRST_CUBE * product(start, first[...])
        applied[0, pl.ds(start, tile), :] = value.astype(jnp.bfloat16)

    def three(start):
        value = product(start, applied[0])
        applied[1, pl.ds(start, tile), :] = value.astype(jnp.bfloat16)

    def four(start):
        rows = applied[1, pl.ds(start, tile), :].astype(jnp.float32)
        third = FIRST_LIN * rows + FIRST_CUBE * product(start, applied[1])
        rows = first[pl.ds(start, tile), :].astype(jnp.float32)
        value = SECOND_LIN * rows + SECOND_CUBE * third
        applied[0, pl.ds(start, tile), :] = value.astype(jnp.bfloat16)

    for step in (one, two, three, four):
        each(step)

    def slot_copy(to, r, w):
        start = pl.multiple_of(own_chunk * width, LANES)
        return pltpu.make_async_remote_copy(
            src_ref=slots.at[rows_at(to, slot_rows), pl.ds(0, w)],
            dst_ref=back_ref.at[mine, :, pl.ds(start, w)],
            send_sem=slot_sems.at[0, r],
            recv_sem=slot_sems.at[1, r],
            device_id=(to, ep),
            device_id_type=MESH,
        )

    def incoming(r, w):
        source = source_of(r)
        start = pl.multiple_of(chunk_of(lax.rem(source, group), core) * width, LANES)
        return pltpu.make_async_remote_copy(
            src_ref=slots.at[rows_at(source, slot_rows), pl.ds(0, w)],
            dst_ref=back_ref.at[source // group, :, pl.ds(start, w)],
            send_sem=slot_sems.at[0, r],
            recv_sem=slot_sems.at[1, r],
            device_id=(source, ep),
            device_id_type=MESH,
        )

    def lay_out(to):
        start = core * (height // 2)
        live = lengths_ref[mine, to]
        for d in range(holders):
            start = start + jnp.where(d < to, lengths_ref[mine, d], 0)
        slot = lax.broadcasted_iota(jnp.int32, (slot_rows, height), 0)
        column = lax.broadcasted_iota(jnp.int32, (slot_rows, height), 1)
        row = slot + start
        row = jnp.where(row >= height, row - height, row)
        row = jnp.where(row >= height, row - height, row)
        chosen = jnp.where(jnp.logical_and(row == column, slot < live), 1.0, 0.0)
        rows = jnp.dot(
            chosen.astype(jnp.bfloat16), applied[0], preferred_element_type=jnp.float32
        )
        slots[rows_at(to, slot_rows), :] = rows.astype(jnp.bfloat16)

    def target_of(r):
        t, k = r // group, r % group
        return lax.rem(mine + t, matrices) * group + lax.rem(place + k, group)

    for r in order:
        to = target_of(r)
        lay_out(to)
        with_width(own_chunk, lambda w, to=to, r=r: slot_copy(to, r, w).start())
    lay_out(dp)

    def keep(w):
        start = pl.multiple_of(own_chunk * width, LANES)
        move = pltpu.make_async_copy(
            slots.at[rows_at(dp, slot_rows), pl.ds(0, w)],
            back_ref.at[mine, :, pl.ds(start, w)],
            local,
        )
        move.start()
        move.wait()

    with_width(own_chunk, keep)

    for r in order:
        to = target_of(r)
        chunk = chunk_of(lax.rem(to, group), core)
        with_width(chunk, lambda w, to=to, r=r: chunk_copy(to, r, w).wait_send())
    for r in [0] + order:
        with_width(own_chunk, lambda w, r=r: core_copy(dp, r, w).wait_send())
    def drain(piece, w):
        for r in range(1, peers):
            term_copy(me, r, piece, w).wait_send()
            block_copy(me, r, piece, w).wait_send()
        for r in range(peers):
            half_copy(me, r, piece, w).wait_send()

    for piece in range(2):
        with_span(piece, core, functools.partial(drain, piece))
    for r in order:
        with_width(own_chunk, lambda w, r=r: slot_copy(dp, r, w).wait_send())
        chunk = chunk_of(lax.rem(source_of(r), group), core)
        with_width(chunk, lambda w, r=r: incoming(r, w).wait_recv())


def orthogonalize(grad, momentum, lengths):
    matrices, slot_rows, columns = grad.shape
    holders, shards = lax.axis_size("dp"), lax.axis_size("ep")
    group = holders // matrices
    peers = group * (shards // 2)
    width = chunk_width(columns, group)
    block = H // BLOCKS
    part = (H // 2 // peers, KEPT * block)
    held = (2, holders * slot_rows, width)
    dma = pltpu.SemaphoreType.DMA
    hbm = pl.BlockSpec(memory_space=pl.ANY)
    vmem = pl.BlockSpec(memory_space=pltpu.VMEM)

    def buffer(*shape):
        return pltpu.VMEM(shape, jnp.bfloat16)

    return pl.pallas_call(
        functools.partial(step_kernel, holders, shards),
        out_shape=(
            pltpu.VMEM(grad.shape, jnp.bfloat16),
            pltpu.VMEM(grad.shape, jnp.float32),
        ),
        in_specs=[pl.BlockSpec(memory_space=pltpu.SMEM), hbm, hbm],
        out_specs=(vmem, vmem),
        scratch_shapes=[
            pltpu.VMEM(grad.shape, jnp.float32),
            pltpu.VMEM(grad.shape, jnp.float32),
            buffer(*grad.shape),
            buffer(*held),
            pltpu.VMEM((H, 2 * width), jnp.float32),
            buffer(H, 2 * width),
            buffer(H // 2, KEPT * block),
            buffer(peers, *part),
            buffer(*part),
            buffer(H, H + (KEPT - 1) * block),
            pltpu.VMEM((8, block), jnp.float32),
            buffer(H, width),
            buffer(2, H, width),
            buffer(holders * slot_rows, width),
            dma((2, holders)),
            dma((2, holders)),
            dma((2, 2, peers)),
            dma((2, 2, peers)),
            dma((2, 2, peers)),
            dma((2,)),
            dma((2, holders)),
            dma((2, matrices)),
            dma,
        ],
        compiler_params=pltpu.CompilerParams(
            collective_id=0, has_side_effects=True, vmem_limit_bytes=VMEM_LIMIT
        ),
        name="orthogonalize",
    )(lengths, grad, momentum)


def chunk_width(columns, group):
    return -(-columns // (group * LANES)) * LANES


def split_body(grad, momentum, lengths):
    back, new_momentum = orthogonalize(grad, momentum, lengths)
    return (new_momentum, back.astype(jnp.float32) * math.sqrt(max(H, D)))


def can_split(holders, shards, matrices, slot_rows, columns):
    if holders % matrices or shards % 2 or slot_rows % 16:
        return False
    group = holders // matrices
    if group * chunk_width(columns, group) * 3 > columns * 4:
        return False
    return H % (BLOCKS * LANES) == 0 and H // 2 % (group * (shards // 2) * 16) == 0


def solution(mesh):
    def run(grad, momentum, lengths):
        matrices, slots, columns = grad.shape
        holders, shards = mesh.shape["dp"], mesh.shape["ep"]
        fits = can_split(holders, shards, matrices, slots // holders, columns // shards)
        return jax.shard_map(
            split_body if fits else gathered_body,
            mesh=mesh,
            in_specs=(P(None, "dp", "ep"), P(None, "dp", "ep"), P()),
            out_specs=(P(None, "dp", "ep"), P(None, "dp", "ep")),
            check_vma=False,
        )(grad, momentum, lengths)

    return run
```

```python
import functools
import math

import jax
import jax.numpy as jnp
from jax import lax
from jax.experimental import pallas as pl
from jax.experimental.pallas import tpu as pltpu
from jax.sharding import PartitionSpec as P

H = 1024
D = 3584


MOMENTUM_COEF = 0.95
EPSILON = 1e-06
FIRST_LIN = 3.0
FIRST_CUBE = -2.5
SECOND_LIN = 1.5
SECOND_CUBE = -0.5

LANES = 128
BLOCKS = 8
KEPT = BLOCKS // 2 + 1
MESH = pl.DeviceIdType.MESH
VMEM_LIMIT = 58 * 1024 * 1024


def from_root(block, axis, owner):
    block = jnp.where(lax.axis_index(axis) == owner, block, jnp.zeros_like(block))
    return lax.psum(block, axis)


def newton_polar(scaled_gram, factor, matrix):
    product = jnp.dot(scaled_gram, matrix, preferred_element_type=jnp.float32)
    first_iter = (factor * (FIRST_LIN * matrix.astype(jnp.float32) + FIRST_CUBE * product)).astype(
        jnp.bfloat16
    )
    product = jnp.dot(scaled_gram, first_iter, preferred_element_type=jnp.float32)
    applied = (FIRST_LIN * first_iter.astype(jnp.float32) + FIRST_CUBE * product).astype(
        jnp.bfloat16
    )
    second = jnp.dot(scaled_gram, applied, preferred_element_type=jnp.float32).astype(jnp.bfloat16)
    third = FIRST_LIN * second.astype(jnp.float32) + FIRST_CUBE * jnp.dot(
        scaled_gram, second, preferred_element_type=jnp.float32
    )
    return (SECOND_LIN * first_iter.astype(jnp.float32) + SECOND_CUBE * third).astype(jnp.bfloat16)


def gathered_body(grad, momentum, lengths):
    matrices = grad.shape[0]
    slot_rows = grad.shape[1]
    columns = grad.shape[2]
    new_momentum = MOMENTUM_COEF * momentum + grad
    rounded = (grad + MOMENTUM_COEF * new_momentum).astype(jnp.bfloat16)
    holders = lax.axis_size("dp")
    myself = lax.axis_index("dp")
    is_owner = myself < matrices
    chosen = jnp.minimum(myself, matrices - 1)
    offsets = jnp.cumsum(lengths, axis=1) - lengths
    chosen_len = lax.dynamic_index_in_dim(lengths, chosen, 0, keepdims=False)
    chosen_off = lax.dynamic_index_in_dim(offsets, chosen, 0, keepdims=False)
    device_ids = jnp.arange(holders, dtype=jnp.int32)
    portion = lax.all_gather(rounded, "dp", axis=1, tiled=True)
    piece_rows = portion.shape[1]
    incoming = lax.dynamic_index_in_dim(portion, chosen, 0, keepdims=False)
    slot_ids = jnp.arange(piece_rows, dtype=jnp.int32)
    source = slot_ids // slot_rows
    within = slot_ids % slot_rows
    matches = source[:, None] == device_ids[None, :]
    length_at = jnp.sum(jnp.where(matches, chosen_len[None, :], 0), axis=1)
    offset_at = jnp.sum(jnp.where(matches, chosen_off[None, :], 0), axis=1)
    keep = jnp.logical_and(within < length_at, is_owner)
    target = jnp.where(keep, offset_at + within, H)
    matrix = jnp.zeros((H, columns), jnp.bfloat16).at[target].set(incoming, mode="drop")
    portion = lax.all_gather(matrix, "ep", axis=1, tiled=True)
    gram_full = jnp.dot(portion, portion.T, preferred_element_type=jnp.float32)
    scale_sq = lax.rsqrt(jnp.sum(gram_full * gram_full) + EPSILON)
    scaled_gram = (scale_sq * gram_full).astype(jnp.bfloat16)
    ortho = newton_polar(scaled_gram, jnp.sqrt(scale_sq), matrix)
    scale_out = math.sqrt(max(H, D))
    positions = jnp.arange(slot_rows, dtype=jnp.int32)
    results = []
    for matrix_id in range(matrices):
        owned_ortho = from_root(ortho, "dp", matrix_id)
        own_length = lax.dynamic_index_in_dim(lengths[matrix_id], myself, 0, keepdims=False)
        own_offset = lax.dynamic_index_in_dim(offsets[matrix_id], myself, 0, keepdims=False)
        is_valid = positions < own_length
        picked = jnp.take(owned_ortho, jnp.where(is_valid, own_offset + positions, 0), axis=0)
        results.append(
            jnp.where(is_valid[:, None], picked.astype(jnp.float32) * scale_out, jnp.float32(0.0))
        )
    return (new_momentum, jnp.stack(results))


def other_core(ep):
    return ep + 1 - 2 * lax.rem(ep, 2)


def rows_at(index, count):
    return pl.ds(pl.multiple_of(index * count, count), count)


def step_kernel(
    holders,
    shards,
    lengths_ref,
    grad_hbm,
    momentum_hbm,
    back_ref,
    fresh_ref,
    grad_ref,
    momentum_ref,
    rounded,
    held,
    packed,
    both,
    parts,
    terms,
    reduced,
    gram,
    squares,
    first,
    applied,
    slots,
    chunk_sems,
    core_sems,
    term_sems,
    block_sems,
    half_sems,
    own_sems,
    slot_sems,
    load_sems,
    local,
):
    matrices, slot_rows, columns = grad_ref.shape
    group = holders // matrices
    chips = shards // 2
    peers = group * chips
    width = held.shape[2]
    narrow = columns - (group - 1) * width
    height = both.shape[0]
    block = height // BLOCKS
    part_rows = height // 2 // peers
    span = KEPT * block

    dp, ep = lax.axis_index("dp"), lax.axis_index("ep")
    core = lax.rem(ep, 2)
    mine = dp // group
    place = lax.rem(dp, group)
    base = dp - place
    sibling = (dp, other_core(ep))

    def chunk_of(index, core):
        return lax.rem(index + core, group)

    def with_width(chunk, use):
        @pl.when(chunk < group - 1)
        def _():
            use(width)

        @pl.when(chunk == group - 1)
        def _():
            use(narrow)

    own_chunk = chunk_of(place, core)
    sibling_chunk = chunk_of(place, 1 - core)

    partners = [(lax.rem(dp + r, holders), ep) for r in range(1, holders)] + [sibling]
    for chip in range(1, chips):
        other = lax.rem(ep // 2 + chip, chips) * 2 + core
        partners += [(base + k, other) for k in range(group)]

    def load(j):
        return [
            pltpu.make_async_copy(source.at[j], target.at[j], load_sems.at[which, j])
            for which, (source, target) in enumerate(
                [(grad_hbm, grad_ref), (momentum_hbm, momentum_ref)]
            )
        ]

    for t in range(1, matrices + 1):
        for copy in load(lax.rem(mine + t, matrices)):
            copy.start()
    if narrow < width:
        held[:, :, narrow:] = jnp.zeros((2, held.shape[1], width - narrow), held.dtype)
    barrier = pltpu.get_barrier_semaphore()
    for partner in partners:
        pl.semaphore_signal(barrier, inc=1, device_id=partner, device_id_type=MESH)

    def round_rows(j):
        for copy in load(j):
            copy.wait()
        momentum = MOMENTUM_COEF * momentum_ref[j] + grad_ref[j]
        fresh_ref[j] = momentum
        rounded[j] = (grad_ref[j] + MOMENTUM_COEF * momentum).astype(rounded.dtype)

    def chunk_copy(to, r, w):
        start = pl.multiple_of(chunk_of(lax.rem(to, group), core) * width, LANES)
        return pltpu.make_async_remote_copy(
            src_ref=rounded.at[to // group, :, pl.ds(start, w)],
            dst_ref=held.at[0, rows_at(dp, slot_rows), pl.ds(0, w)],
            send_sem=chunk_sems.at[0, r],
            recv_sem=chunk_sems.at[1, r],
            device_id=(to, ep),
            device_id_type=MESH,
        )

    def core_copy(source, r, w):
        return pltpu.make_async_remote_copy(
            src_ref=held.at[0, rows_at(source, slot_rows), pl.ds(0, w)],
            dst_ref=held.at[1, rows_at(source, slot_rows), pl.ds(0, w)],
            send_sem=core_sems.at[0, r],
            recv_sem=core_sems.at[1, r],
            device_id=sibling,
            device_id_type=MESH,
        )

    round_rows(lax.rem(mine + 1, matrices))
    pl.semaphore_wait(barrier, len(partners))
    order = []
    for t in range(1, matrices + 1):
        if t > 1:
            round_rows(lax.rem(mine + t, matrices))
        for k in range(group):
            if t == matrices and k == 0:
                continue
            order.append((t % matrices) * group + k)
            to = lax.rem(mine + t, matrices) * group + lax.rem(place + k, group)
            r = order[-1]
            chunk = chunk_of(lax.rem(to, group), core)
            with_width(chunk, lambda w, to=to, r=r: chunk_copy(to, r, w).start())

    def own_move(w):
        start = pl.multiple_of(own_chunk * width, LANES)
        move = pltpu.make_async_copy(
            rounded.at[mine, :, pl.ds(start, w)],
            held.at[0, rows_at(dp, slot_rows), pl.ds(0, w)],
            local,
        )
        move.start()
        move.wait()

    with_width(own_chunk, own_move)
    with_width(own_chunk, lambda w: core_copy(dp, 0, w).start())

    def source_of(r):
        t, k = r // group, r % group
        half = lax.rem(mine + matrices - t, matrices)
        return half * group + lax.rem(place + group - k, group)

    def first_row(holder):
        row = core * (height // 2)
        for d in range(holders):
            row = row + jnp.where(d < holder, lengths_ref[mine, d], 0)
        return row

    tile = 512
    half_slots = group * slot_rows

    def pack(half, open_sum, close_sum):
        slot = lax.broadcasted_iota(jnp.int32, (1, half_slots), 1)
        target = jnp.full((1, half_slots), -1, jnp.int32)
        for k in range(group):
            start = first_row(half * group + k)
            live = lengths_ref[mine, half * group + k]
            inside = jnp.logical_and(slot >= k * slot_rows, slot < k * slot_rows + live)
            row = slot - k * slot_rows + start
            target = jnp.where(inside, jnp.where(row >= height, row - height, row), target)

        def run(step, carry):
            start = pl.multiple_of(step * tile, tile)
            rows = lax.broadcasted_iota(jnp.int32, (tile, half_slots), 0) + start
            chosen = jnp.where(rows == target, 1.0, 0.0).astype(jnp.bfloat16)
            for which in range(2):
                at = pl.ds(start, tile), pl.ds(which * width, width)
                value = jnp.dot(
                    chosen,
                    held[which, rows_at(half, half_slots), :],
                    preferred_element_type=jnp.float32,
                )
                if not open_sum:
                    value = value + packed[at]
                if close_sum:
                    both[at] = value.astype(jnp.bfloat16)
                else:
                    packed[at] = value
            return carry

        lax.fori_loop(0, height // tile, run, 0)

    for t in range(matrices):
        arrivals = [r for r in order if r // group == t]
        for r in arrivals:

            def pass_on(w, r=r):
                chunk_copy(dp, r, w).wait_recv()
                core_copy(source_of(r), r, w).start()

            with_width(own_chunk, pass_on)
        for r in ([0] if t == 0 else []) + arrivals:
            with_width(sibling_chunk, lambda w, r=r: core_copy(dp, r, w).wait_recv())
        pack(lax.rem(mine + matrices - t, matrices), t == 0, t == matrices - 1)

    me = place * chips + ep // 2

    def device(index):
        return (base + index // chips, lax.rem(index, chips) * 2 + core)

    split = 2 * block

    def with_span(piece, of_core, use):
        if piece == 0:
            use(split)
            return

        @pl.when(of_core == 0)
        def _():
            use(span - split)

        @pl.when(of_core != 0)
        def _():
            use(span - block - split)

    def term_copy(to, r, piece, w):
        return pltpu.make_async_remote_copy(
            src_ref=parts.at[rows_at(to, part_rows), pl.ds(piece * split, w)],
            dst_ref=terms.at[r, :, pl.ds(piece * split, w)],
            send_sem=term_sems.at[0, piece, r],
            recv_sem=term_sems.at[1, piece, r],
            device_id=device(to),
            device_id_type=MESH,
        )

    owners = block // part_rows
    for t in range(1, BLOCKS // 2 + 1):
        row = lax.rem(me // owners + t, BLOCKS // 2)
        start = pl.multiple_of(row * block, block)
        part = lax.dot_general(
            both[pl.ds(start, block), :],
            both[pl.ds(start, span), :],
            (((1,), (1,)), ((), ())),
            preferred_element_type=jnp.float32,
        )
        parts[pl.ds(start, block), :] = part.astype(jnp.bfloat16)
        for k in range(owners):
            if t == BLOCKS // 2 and k == 0:
                continue
            to = row * owners + lax.rem(me + k, owners)
            term_copy(to, lax.rem(to + peers - me, peers), 0, split).start()
    for r in range(1, peers):
        to = lax.rem(me + r, peers)
        with_span(1, core, lambda w, to=to, r=r: term_copy(to, r, 1, w).start())

    def blocks_at(index, half, piece, w):
        row = half * (height // 2) + index * part_rows
        column = pl.multiple_of(row // block * block, block) + piece * split
        return gram.at[
            pl.ds(pl.multiple_of(row, part_rows), part_rows),
            pl.ds(pl.multiple_of(column, block), w),
        ]

    bits = [1 << b for b in range(peers.bit_length() - 1)]
    passes = {}
    if len(bits) > 2:
        passes = {bit: bit + bits[(b + 1) % len(bits)] for b, bit in enumerate(bits)}
    direct = bits + [m for m in range(1, peers) if m not in bits and m not in passes.values()]

    def flip(mask):
        other = me
        for bit in bits:
            if mask & bit:
                other = other + bit * (1 - 2 * lax.rem(me // bit, 2))
        return other

    def block_copy(source, to, r, piece, w):
        there = blocks_at(source, 0, piece, w)
        return pltpu.make_async_remote_copy(
            src_ref=reduced.at[:, pl.ds(piece * split, w)] if source is me else there,
            dst_ref=there,
            send_sem=block_sems.at[0, piece, r],
            recv_sem=block_sems.at[1, piece, r],
            device_id=device(to),
            device_id_type=MESH,
        )

    def half_copy(source, r, piece, w):
        own = reduced.at[:, pl.ds(piece * split, w)]
        return pltpu.make_async_remote_copy(
            src_ref=own if r == 0 else blocks_at(source, 0, piece, w),
            dst_ref=blocks_at(source, 1, piece, w),
            send_sem=half_sems.at[0, piece, r],
            recv_sem=half_sems.at[1, piece, r],
            device_id=sibling,
            device_id_type=MESH,
        )

    def own_copy(piece, w):
        return pltpu.make_async_copy(
            reduced.at[:, pl.ds(piece * split, w)], blocks_at(me, 0, piece, w), own_sems.at[piece]
        )

    def reduce_piece(piece, w):
        at = pl.ds(piece * split, w)
        total = parts[rows_at(me, part_rows), at].astype(jnp.float32)
        for r in range(1, peers):
            term_copy(me, r, piece, w).wait_recv()
            total = total + terms[r, :, at].astype(jnp.float32)
        reduced[:, at] = total.astype(reduced.dtype)
        for mask in direct:
            block_copy(me, flip(mask), mask, piece, w).start()
        half_copy(me, 0, piece, w).start()
        own_copy(piece, w).start()

    def forward_piece(piece, w):
        for mask in direct + sorted(passes.values()):
            source = flip(mask)
            block_copy(me, me, mask, piece, w).wait_recv()
            half_copy(source, mask, piece, w).start()
            if mask in passes:
                block_copy(source, flip(passes[mask] - mask), passes[mask], piece, w).start()
        own_copy(piece, w).wait()

    def await_half(piece, w):
        for r in range(peers):
            half_copy(me, r, piece, w).wait_recv()

    def assemble(half, blocks):
        for i in range(half * BLOCKS // 2, (half + 1) * BLOCKS // 2):
            for k in blocks:

                def place(i=i, k=k):
                    j = (i + k) % BLOCKS
                    piece = gram[pl.ds(i * block, block), pl.ds((i + k) * block, block)]
                    if i + k >= BLOCKS:
                        gram[pl.ds(i * block, block), pl.ds(j * block, block)] = piece
                    if k > 0:
                        gram[pl.ds(j * block, block), pl.ds(i * block, block)] = piece.T
                    wide = piece.astype(jnp.float32)
                    square = (wide * wide).reshape(-1, 8, block).sum(axis=0)
                    squares[...] += (2.0 if k > 0 else 1.0) * square

                if k == KEPT - 1:
                    pl.when(core == half)(place)
                else:
                    place()

    squares[...] = jnp.zeros(squares.shape, squares.dtype)
    for piece in range(2):
        with_span(piece, core, functools.partial(reduce_piece, piece))
    for piece, blocks in ((0, range(2)), (1, range(2, KEPT))):
        with_span(piece, core, functools.partial(forward_piece, piece))
        assemble(0, blocks)
        with_span(piece, 1 - core, functools.partial(await_half, piece))
        assemble(1, blocks)
    scale_sq = lax.rsqrt(jnp.sum(squares[...], keepdims=True) + EPSILON)
    factor = jnp.sqrt(scale_sq)

    def product(start, right):
        return scale_sq * jnp.dot(
            gram[pl.ds(start, tile), :height], right, preferred_element_type=jnp.float32
        )

    def each(step):
        def run(index, carry):
            step(pl.multiple_of(index * tile, tile))
            return carry

        lax.fori_loop(0, height // tile, run, 0)

    def one(start):
        rows = both[pl.ds(start, tile), :width].astype(jnp.float32)
        value = factor * (FIRST_LIN * rows + FIRST_CUBE * product(start, both[:, :width]))
        first[pl.ds(start, tile), :] = value.astype(jnp.bfloat16)

    def two(start):
        rows = first[pl.ds(start, tile), :].astype(jnp.float32)
        value = FIRST_LIN * rows + FIRST_CUBE * product(start, first[...])
        applied[0, pl.ds(start, tile), :] = value.astype(jnp.bfloat16)

    def three(start):
        value = product(start, applied[0])
        applied[1, pl.ds(start, tile), :] = value.astype(jnp.bfloat16)

    def four(start):
        rows = applied[1, pl.ds(start, tile), :].astype(jnp.float32)
        third = FIRST_LIN * rows + FIRST_CUBE * product(start, applied[1])
        rows = first[pl.ds(start, tile), :].astype(jnp.float32)
        value = SECOND_LIN * rows + SECOND_CUBE * third
        applied[0, pl.ds(start, tile), :] = value.astype(jnp.bfloat16)

    for step in (one, two, three, four):
        each(step)

    def slot_copy(to, r, w):
        start = pl.multiple_of(own_chunk * width, LANES)
        return pltpu.make_async_remote_copy(
            src_ref=slots.at[rows_at(to, slot_rows), pl.ds(0, w)],
            dst_ref=back_ref.at[mine, :, pl.ds(start, w)],
            send_sem=slot_sems.at[0, r],
            recv_sem=slot_sems.at[1, r],
            device_id=(to, ep),
            device_id_type=MESH,
        )

    def incoming(r, w):
        source = source_of(r)
        start = pl.multiple_of(chunk_of(lax.rem(source, group), core) * width, LANES)
        return pltpu.make_async_remote_copy(
            src_ref=slots.at[rows_at(source, slot_rows), pl.ds(0, w)],
            dst_ref=back_ref.at[source // group, :, pl.ds(start, w)],
            send_sem=slot_sems.at[0, r],
            recv_sem=slot_sems.at[1, r],
            device_id=(source, ep),
            device_id_type=MESH,
        )

    def lay_out(to):
        start = core * (height // 2)
        live = lengths_ref[mine, to]
        for d in range(holders):
            start = start + jnp.where(d < to, lengths_ref[mine, d], 0)
        slot = lax.broadcasted_iota(jnp.int32, (slot_rows, height), 0)
        column = lax.broadcasted_iota(jnp.int32, (slot_rows, height), 1)
        row = slot + start
        row = jnp.where(row >= height, row - height, row)
        row = jnp.where(row >= height, row - height, row)
        chosen = jnp.where(jnp.logical_and(row == column, slot < live), 1.0, 0.0)
        rows = jnp.dot(
            chosen.astype(jnp.bfloat16), applied[0], preferred_element_type=jnp.float32
        )
        slots[rows_at(to, slot_rows), :] = rows.astype(jnp.bfloat16)

    def target_of(r):
        t, k = r // group, r % group
        return lax.rem(mine + t, matrices) * group + lax.rem(place + k, group)

    for r in order:
        to = target_of(r)
        lay_out(to)
        with_width(own_chunk, lambda w, to=to, r=r: slot_copy(to, r, w).start())
    lay_out(dp)

    def keep(w):
        start = pl.multiple_of(own_chunk * width, LANES)
        move = pltpu.make_async_copy(
            slots.at[rows_at(dp, slot_rows), pl.ds(0, w)],
            back_ref.at[mine, :, pl.ds(start, w)],
            local,
        )
        move.start()
        move.wait()

    with_width(own_chunk, keep)

    for r in order:
        to = target_of(r)
        chunk = chunk_of(lax.rem(to, group), core)
        with_width(chunk, lambda w, to=to, r=r: chunk_copy(to, r, w).wait_send())
    for r in [0] + order:
        with_width(own_chunk, lambda w, r=r: core_copy(dp, r, w).wait_send())
    def drain(piece, w):
        for r in range(1, peers):
            term_copy(me, r, piece, w).wait_send()
            block_copy(me, me, r, piece, w).wait_send()
        for r in range(peers):
            half_copy(me, r, piece, w).wait_send()

    for piece in range(2):
        with_span(piece, core, functools.partial(drain, piece))
    for r in order:
        with_width(own_chunk, lambda w, r=r: slot_copy(dp, r, w).wait_send())
        chunk = chunk_of(lax.rem(source_of(r), group), core)
        with_width(chunk, lambda w, r=r: incoming(r, w).wait_recv())


def orthogonalize(grad, momentum, lengths):
    matrices, slot_rows, columns = grad.shape
    holders, shards = lax.axis_size("dp"), lax.axis_size("ep")
    group = holders // matrices
    peers = group * (shards // 2)
    width = chunk_width(columns, group)
    block = H // BLOCKS
    part = (H // 2 // peers, KEPT * block)
    held = (2, holders * slot_rows, width)
    dma = pltpu.SemaphoreType.DMA
    hbm = pl.BlockSpec(memory_space=pl.ANY)
    vmem = pl.BlockSpec(memory_space=pltpu.VMEM)

    def buffer(*shape):
        return pltpu.VMEM(shape, jnp.bfloat16)

    return pl.pallas_call(
        functools.partial(step_kernel, holders, shards),
        out_shape=(
            pltpu.VMEM(grad.shape, jnp.bfloat16),
            pltpu.VMEM(grad.shape, jnp.float32),
        ),
        in_specs=[pl.BlockSpec(memory_space=pltpu.SMEM), hbm, hbm],
        out_specs=(vmem, vmem),
        scratch_shapes=[
            pltpu.VMEM(grad.shape, jnp.float32),
            pltpu.VMEM(grad.shape, jnp.float32),
            buffer(*grad.shape),
            buffer(*held),
            pltpu.VMEM((H, 2 * width), jnp.float32),
            buffer(H, 2 * width),
            buffer(H // 2, KEPT * block),
            buffer(peers, *part),
            buffer(*part),
            buffer(H, H + (KEPT - 1) * block),
            pltpu.VMEM((8, block), jnp.float32),
            buffer(H, width),
            buffer(2, H, width),
            buffer(holders * slot_rows, width),
            dma((2, holders)),
            dma((2, holders)),
            dma((2, 2, peers)),
            dma((2, 2, peers)),
            dma((2, 2, peers)),
            dma((2,)),
            dma((2, holders)),
            dma((2, matrices)),
            dma,
        ],
        compiler_params=pltpu.CompilerParams(
            collective_id=0, has_side_effects=True, vmem_limit_bytes=VMEM_LIMIT
        ),
        name="orthogonalize",
    )(lengths, grad, momentum)


def chunk_width(columns, group):
    return -(-columns // (group * LANES)) * LANES


def split_body(grad, momentum, lengths):
    back, new_momentum = orthogonalize(grad, momentum, lengths)
    return (new_momentum, back.astype(jnp.float32) * math.sqrt(max(H, D)))


def can_split(holders, shards, matrices, slot_rows, columns):
    if holders % matrices or shards % 2 or slot_rows % 16:
        return False
    group = holders // matrices
    peers = group * (shards // 2)
    if peers & (peers - 1):
        return False
    if group * chunk_width(columns, group) * 3 > columns * 4:
        return False
    return H % (BLOCKS * LANES) == 0 and H // 2 % (peers * 16) == 0


def solution(mesh):
    def run(grad, momentum, lengths):
        matrices, slots, columns = grad.shape
        holders, shards = mesh.shape["dp"], mesh.shape["ep"]
        fits = can_split(holders, shards, matrices, slots // holders, columns // shards)
        return jax.shard_map(
            split_body if fits else gathered_body,
            mesh=mesh,
            in_specs=(P(None, "dp", "ep"), P(None, "dp", "ep"), P()),
            out_specs=(P(None, "dp", "ep"), P(None, "dp", "ep")),
            check_vma=False,
        )(grad, momentum, lengths)

    return run
```
